512 devices in a mesh: rel: 32 (over z, core), rep: 16 (over y, x).
Axes of the slice: x: 4, y: 4, z: 16, core: 2. Of those that a mesh axis runs over, the one named last changes fastest.
Arguments:
- core: bfloat16 [512, 128, 512], P('rel'), may hold values from -0.0234375 to 0.0234375
- rel_emb: bfloat16 [64, 128], replicated, may hold values from -0.5 to 0.5
- ents: bfloat16 [65536, 512], P(('rel', 'rep')), may hold values from -6 to 6
- pool: bfloat16 [256, 512], replicated, may hold values from -6 to 6
- owner_of: int32 [64], replicated, may hold values from 0 to 31, as said below
- rel_ids: int32 [524288], P(('rel', 'rep')), may hold values from 0 to 63, as said below
- head_ids: int32 [524288], P(('rel', 'rep')), may hold values from 0 to 127
- tail_ids: int32 [524288], P(('rel', 'rep')), may hold values from 0 to 127
- fill: int32 [512, 32], P(('rel', 'rep')), may hold values from 0 to 32, as said below
Outputs:
- core_grad: bfloat16 [512, 128, 512], P('rel')
- rel_grad: float32 [64, 128], replicated
- ent_grad: bfloat16 [65536, 512], P(('rel', 'rep'))
- pool_grad: bfloat16 [256, 512], replicated
The draws below stay inside these ranges and needn't reach their ends.
Inputs may be any that keep to these rules, and one draw needn't show every extreme that they name: `owner_of`: every owner index names exactly 2 relations. `rel_ids`: every slot of a device's block o, used or not, names a relation whose owner is o. `fill`: some block is full in every draw.
All inputs are finite; a program needn't handle non-finite values.
Results may differ from the reference program's by a relative error of at most 0.019.
Values may be sent and summed in bfloat16 or wider, within the bound.
No kernel may reach another device: no remote copies, remote signals or barrier semaphores. Data moves between devices by JAX's collectives and lax.ppermute only.
A program may use at most 64 MiB of HBM per device.

```python
import jax
import jax.numpy as jnp
from jax import lax

DE = 512
DR = 128
CAP = 32
REL_DEV = 2
ENT_DEV = 128
POOL = 256
RELS = 64
ENTS = 65536
SLOTS = 524288
N_REL = 32
N_REP = 16


def owner_perm(key):
    return jax.random.permutation(key, RELS)


def draw_owner_of(key, part):
    perm = owner_perm(key)
    owners = jnp.arange(RELS, dtype=jnp.int32) // REL_DEV
    return jnp.zeros((RELS,), jnp.int32).at[perm].set(owners)


def draw_rel_ids(key, part):
    perm = owner_perm(key)
    key = jax.random.fold_in(key, 12)
    pick = jax.random.randint(key, (N_REL * N_REP, N_REL, CAP), 0, REL_DEV)
    owner = jnp.arange(N_REL, dtype=jnp.int32)[None, :, None]
    return jnp.take(perm, owner * REL_DEV + pick).reshape(-1).astype(jnp.int32)


def draw_fill(key, part):
    key = jax.random.fold_in(key, 13)
    first, second, third = jax.random.split(key, 3)
    weight = jax.random.randint(first, (N_REL,), 1, 5)
    hot = jax.random.randint(second, (), 0, N_REL)
    base = jax.random.randint(third, (N_REL * N_REP, N_REL), CAP // 2, CAP + 1)
    load = jnp.minimum(CAP, weight[None, :] * base // 4)
    owners = jnp.arange(N_REL, dtype=jnp.int32)[None, :]
    return jnp.where(owners == hot, CAP, load).astype(jnp.int32)


def with_ends(values, stream_key, smallest, top_value):
    spot = [jax.random.randint(jax.random.fold_in(stream_key, axis), (), 0, length) for axis, length in enumerate(values.shape)]
    widest = values.shape.index(max(values.shape))
    neighbour = spot[:widest] + [(spot[widest] + 1) % values.shape[widest]] + spot[widest + 1:]
    return values.at[tuple(spot)].set(smallest).at[tuple(neighbour)].set(top_value)


def block_levels(rng, shape, shards, low, high):
    factor_of, own = 1.0, jax.random.fold_in(rng, 6)
    for dim, parts in shards:
        draws = jnp.exp(jax.random.uniform(jax.random.fold_in(own, dim), (parts,), jnp.float32, low / len(shards), high / len(shards)))
        factor_of = factor_of * jnp.repeat(draws, shape[dim] // parts).reshape([-1 if axis == dim else 1 for axis in range(len(shape))])
    return factor_of


def scatter_about(rng, extent, spread, most, shards=(), held_as=jnp.bfloat16):
    values = jax.random.normal(rng, extent, jnp.float32) * spread
    if len(shards) > 0:
        values = block_levels(rng, extent, shards, -0.22, 0.18) * values
    return jnp.clip(values, min=-most, max=most).astype(held_as)


def setup_inputs(seed: int = 0) -> dict:
    seeds = jax.random.split(jax.random.key(seed), 10)
    core = scatter_about(seeds[0], (DE, DR, DE), (DE * DE // 4) ** -0.5, 0.0234375, ((0, 32),))
    rel_emb = scatter_about(seeds[1], (RELS, DR), DR ** -0.5, 0.5)
    ents = scatter_about(seeds[2], (ENTS, DE), 1.0, 6.0, ((0, 512),))
    pool = scatter_about(seeds[3], (POOL, DE), 1.0, 6.0)
    owner_of = draw_owner_of(jax.random.fold_in(seeds[9], 71), 0)
    rel_ids = draw_rel_ids(jax.random.fold_in(seeds[9], 71), 0)
    head_ids = with_ends(jax.random.randint(seeds[6], (SLOTS,), 0, ENT_DEV), jax.random.fold_in(seeds[6], 1), 0, ENT_DEV - 1).astype(jnp.int32)
    tail_ids = with_ends(jax.random.randint(seeds[7], (SLOTS,), 0, ENT_DEV), jax.random.fold_in(seeds[7], 1), 0, ENT_DEV - 1).astype(jnp.int32)
    fill = draw_fill(jax.random.fold_in(seeds[9], 71), 0)
    return {"core": core, "rel_emb": rel_emb, "ents": ents, "pool": pool, "owner_of": owner_of, "rel_ids": rel_ids, "head_ids": head_ids, "tail_ids": tail_ids, "fill": fill}


def order_tables(owner_of, per_owner):
    count = owner_of.shape[0]
    index = jnp.arange(count, dtype=jnp.int32)
    same = owner_of[:, None] == owner_of[None, :]
    rank = jnp.sum((same & (index[None, :] < index[:, None])).astype(jnp.int32), axis=1)
    return rank, owner_of * per_owner + rank


def forward(rows, select, mats):
    query = jnp.zeros((rows.shape[0], mats.shape[2]), jnp.float32)
    for which in range(mats.shape[0]):
        query = query + select[:, which:which + 1].astype(jnp.float32) * jnp.dot(rows, mats[which], preferred_element_type=jnp.float32)
    return query.astype(jnp.bfloat16)


def backward(rows, select, dquery, mats):
    dhead = jnp.zeros((rows.shape[0], mats.shape[1]), jnp.float32)
    pieces = []
    for which in range(mats.shape[0]):
        mask = select[:, which:which + 1].astype(jnp.float32)
        dhead = dhead + mask * lax.dot_general(dquery, mats[which], (((1,), (1,)), ((), ())), preferred_element_type=jnp.float32)
        masked = (mask * dquery.astype(jnp.float32)).astype(jnp.bfloat16)
        pieces.append(lax.dot_general(rows, masked, (((0,), (0,)), ((), ())), preferred_element_type=jnp.float32).astype(jnp.bfloat16))
    return dhead.astype(jnp.bfloat16), jnp.stack(pieces)


def score(query, tails, used, pool, scale):
    qfloat = query.astype(jnp.float32)
    positive = jnp.sum(qfloat * tails.astype(jnp.float32), axis=1)
    negative = lax.dot_general(query, pool, (((1,), (1,)), ((), ())), preferred_element_type=jnp.float32)
    gpos = -jax.nn.sigmoid(-positive) * used * scale
    gneg = (jax.nn.sigmoid(negative) * (used * scale / pool.shape[0])[:, None]).astype(jnp.bfloat16)
    dquery = (gpos[:, None] * tails.astype(jnp.float32) + jnp.dot(gneg, pool, preferred_element_type=jnp.float32)).astype(jnp.bfloat16)
    dtail = (gpos[:, None] * qfloat).astype(jnp.bfloat16)
    dpool = lax.dot_general(gneg, query, (((0,), (0,)), ((), ())), preferred_element_type=jnp.float32)
    return dquery, dtail, dpool


def reference(core, rel_emb, ents, pool, owner_of, rel_ids, head_ids, tail_ids, fill):
    rank, slot_of = order_tables(owner_of, REL_DEV)
    qindex = jnp.arange(RELS, dtype=jnp.int32)
    order_sel = (slot_of[None, :] == qindex[:, None]).astype(jnp.bfloat16)
    ordered = jnp.dot(order_sel, rel_emb, preferred_element_type=jnp.float32).astype(jnp.bfloat16)
    core32 = core.astype(jnp.float32)
    mats = jnp.einsum("qk,akb->qab", ordered.astype(jnp.float32), core32).astype(jnp.bfloat16)
    mats = mats.reshape(N_REL, REL_DEV, DE, DE)
    shape4 = (N_REL, N_REP, N_REL, CAP)
    heads_all = head_ids.reshape(shape4)
    tails_all = tail_ids.reshape(shape4)
    rels_all = rel_ids.reshape(shape4)
    fill_all = fill.reshape(N_REL, N_REP, N_REL)
    ents4 = ents.reshape(N_REL, N_REP, ENT_DEV, DE)
    scale = 1.0 / N_REP

    def swap_major(array):
        rest = array.shape[2:]
        return jnp.swapaxes(array.reshape((N_REL, N_REL, CAP) + rest), 0, 1).reshape((N_REL, N_REL * CAP) + rest)

    def group(carry, g):
        hid = lax.dynamic_index_in_dim(heads_all, g, 1, keepdims=False).reshape(N_REL, N_REL * CAP)
        tid = lax.dynamic_index_in_dim(tails_all, g, 1, keepdims=False).reshape(N_REL, N_REL * CAP)
        rid = lax.dynamic_index_in_dim(rels_all, g, 1, keepdims=False)
        limit = lax.dynamic_index_in_dim(fill_all, g, 1, keepdims=False)
        block = lax.dynamic_index_in_dim(ents4, g, 1, keepdims=False)
        heads = jax.vmap(lambda table, idx: jnp.take(table, idx, axis=0))(block, hid)
        tails = jax.vmap(lambda table, idx: jnp.take(table, idx, axis=0))(block, tid)
        position = jnp.arange(CAP, dtype=jnp.int32)
        used = (position[None, None, :] < limit[:, :, None]).astype(jnp.float32)
        rank_slot = jnp.take(rank, rid)
        select = (used[..., None] * (rank_slot[..., None] == jnp.arange(REL_DEV, dtype=jnp.int32)).astype(jnp.float32)).astype(jnp.bfloat16)
        xo = swap_major(heads)
        to = swap_major(tails)
        so = swap_major(select.reshape(N_REL, N_REL * CAP, REL_DEV))
        vo = swap_major(used.reshape(N_REL, N_REL * CAP))

        def owner_work(items):
            rows, tail_rows, sel, live, owned = items
            query = forward(rows, sel, owned)
            dquery, dtail, dpool = score(query, tail_rows, live, pool, scale)
            dhead, dmats = backward(rows, sel, dquery, owned)
            return dhead, dtail, dmats, dpool

        dhead, dtail, dmats, dpool = lax.map(owner_work, (xo, to, so, vo, mats))
        dmats = dmats.reshape(RELS, DE, DE).astype(jnp.float32)
        dhs = swap_major(dhead)
        dts = swap_major(dtail)

        def scatter_rows(hrow, trow, dh, dt):
            total = jnp.zeros((ENT_DEV, DE), jnp.float32).at[hrow].add(dh.astype(jnp.float32)).at[trow].add(dt.astype(jnp.float32))
            return total.astype(jnp.bfloat16)

        entg = jax.vmap(scatter_rows)(hid, tid, dhs, dts)
        return (carry[0] + dmats, carry[1] + jnp.sum(dpool, axis=0)), entg

    init = (jnp.zeros((RELS, DE, DE), jnp.float32), jnp.zeros((POOL, DE), jnp.float32))
    sums, entg = lax.scan(group, init, jnp.arange(N_REP, dtype=jnp.int32))
    dmats_sum = sums[0]
    core_grad = jnp.einsum("qk,qab->akb", ordered.astype(jnp.float32), dmats_sum, precision=lax.Precision.HIGHEST).astype(jnp.bfloat16)
    ograd = jnp.einsum("qab,akb->qk", dmats_sum, core32, precision=lax.Precision.HIGHEST)
    rel_grad = jnp.dot(order_sel.astype(jnp.float32).T, ograd, precision=lax.Precision.HIGHEST)
    ent_grad = jnp.swapaxes(entg, 0, 1).reshape(ENTS, DE)
    return core_grad, rel_grad, ent_grad, sums[1].astype(jnp.bfloat16)
```

```python
import jax
import jax.numpy as jnp
from jax import lax
from jax.sharding import Mesh, PartitionSpec as P

ZH, ZL, CORES, REPS = 4, 4, 2, 16
Z = ZH * ZL
REL = ("zh", "zl", "core")
REP = ("y", "x")
LINE = ("zh", "zl")
NEAR = (1, 2, 3)
EXTRA = 16
F32 = jnp.float32
BF16 = jnp.bfloat16


def order_tables(owner_of, per_owner):
    count = owner_of.shape[0]
    index = jnp.arange(count, dtype=jnp.int32)
    same = owner_of[:, None] == owner_of[None, :]
    rank = jnp.sum((same & (index[None, :] < index[:, None])).astype(jnp.int32), axis=1)
    return (rank, owner_of * per_owner + rank)


def exchange(blocks, axis):
    return lax.all_to_all(blocks, axis, split_axis=0, concat_axis=0, tiled=True)


def spread(block, axis, count):
    return exchange(jnp.broadcast_to(block[None], (count,) + block.shape), axis)


def near_step(near):
    pairs = []
    for z in range(Z):
        for core in range(CORES):
            step = {1: 1, 2: 2 if core == 0 else -2, 3: -1}[near]
            pairs.append((z * CORES + core, (z + step) % Z * CORES + core))
    return pairs


def swap_core(block):
    return lax.ppermute(block, "core", [(0, 1), (1, 0)])


def body(core, rel_emb, ents, pool, owner_of, rel_ids, head_ids, tail_ids, fill):
    rels, feats_rel = rel_emb.shape
    rows_dev, _, feats = core.shape
    owners = fill.shape[1]
    cap = rel_ids.shape[0] // owners
    per_owner = rels // owners
    own = owners // REPS
    mine = own * per_owner
    seats = own * cap
    ent_rows = ents.shape[0]
    pool_rows = pool.shape[0]
    scale = 1.0 / REPS
    g = lax.axis_index(REP)
    zl = lax.axis_index("zl")
    c = lax.axis_index("core")

    rank, slot_of = order_tables(owner_of, per_owner)
    qindex = jnp.arange(rels, dtype=jnp.int32)
    order_sel = (slot_of[None, :] == qindex[:, None]).astype(BF16)
    ordered = jnp.dot(order_sel, rel_emb, preferred_element_type=F32).astype(BF16)

    own_rows = lax.dynamic_slice_in_dim(ordered, g * mine, mine, 0)
    part = jnp.einsum("wk,akb->wab", own_rows, core, preferred_element_type=F32).astype(BF16)
    far = spread(part, "zh", ZH)
    near = [far] + [lax.ppermute(far, REL, near_step(s)) for s in NEAR]
    half = jnp.stack(near)
    half = jnp.take(half, (zl - jnp.arange(ZL)) % ZL, axis=0)
    other = swap_core(half)
    both = jnp.where(c == 0, jnp.stack([half, other]), jnp.stack([other, half]))
    mats = jnp.transpose(both, (3, 2, 1, 0, 4, 5)).reshape(own, per_owner * feats, feats)

    relhot = rel_ids[None, :] == jnp.arange(rels, dtype=jnp.int32)[:, None]
    rank_slot = jnp.sum(jnp.where(relhot, rank[:, None], 0), axis=0)
    used = (jnp.arange(cap, dtype=jnp.int32)[None, :] < fill[0][:, None]).astype(jnp.int32)
    numbers = jnp.concatenate(
        [a.reshape(REPS, seats) for a in (head_ids, tail_ids, rank_slot, used)], axis=1
    ).astype(BF16)
    numbers = jnp.pad(numbers[:, None, :], ((0, 0), (0, EXTRA - 1), (0, feats - 4 * seats)))
    sent = jnp.concatenate(
        [jnp.broadcast_to(ents[None], (REPS, ent_rows, feats)), numbers], axis=1
    )
    got = exchange(sent, REP)
    table = got[:, :ent_rows]
    line = got[:, ent_rows].astype(jnp.int32)
    hot = (
        line[:, None, : 2 * seats] == jnp.arange(ent_rows, dtype=jnp.int32)[None, :, None]
    ).astype(BF16)
    rows = jnp.einsum("sen,sef->snf", hot, table, preferred_element_type=F32).astype(BF16)

    def by_owner(a):
        a = a.reshape((REPS, own, cap) + a.shape[2:])
        return jnp.swapaxes(a, 0, 1).reshape((own, REPS * cap) + a.shape[3:])

    def by_source(a):
        a = a.reshape((own, REPS, cap) + a.shape[2:])
        return jnp.swapaxes(a, 0, 1).reshape((REPS, seats) + a.shape[3:])

    heads = by_owner(rows[:, :seats])
    tails = by_owner(rows[:, seats:])
    rank_got = by_owner(line[:, 2 * seats : 3 * seats])
    live = by_owner(line[:, 3 * seats : 4 * seats]).astype(F32)
    mask = [live * (rank_got == w).astype(F32) for w in range(per_owner)]
    masks = [m[..., None].astype(BF16) for m in mask]
    heads_wide = jnp.concatenate([m * heads for m in masks], axis=-1)

    query = jnp.einsum("oni,oif->onf", heads_wide, mats, preferred_element_type=F32).astype(BF16)
    qfloat = query.astype(F32)
    positive = jnp.sum(qfloat * tails.astype(F32), axis=-1)
    negative = jnp.einsum("onf,pf->onp", query, pool, preferred_element_type=F32)
    gpos = -jax.nn.sigmoid(-positive) * live * scale
    gneg = (jax.nn.sigmoid(negative) * (live * scale / pool_rows)[..., None]).astype(BF16)
    dquery = (
        gpos[..., None] * tails.astype(F32)
        + jnp.einsum("onp,pf->onf", gneg, pool, preferred_element_type=F32)
    ).astype(BF16)
    dtail = (gpos[..., None] * qfloat).astype(BF16)
    dpool = jnp.einsum("onp,onf->pf", gneg, query, preferred_element_type=F32).astype(BF16)
    dmats = jnp.einsum("oni,onf->oif", heads_wide, dquery, preferred_element_type=F32)

    dm = dmats.reshape(mine, ZH, ZL, CORES, rows_dev, feats)
    dm = jnp.transpose(dm, (3, 2, 1, 0, 4, 5))
    kept = lax.dynamic_index_in_dim(dm, c, 0, keepdims=False)
    given = lax.dynamic_index_in_dim(dm, 1 - c, 0, keepdims=False).astype(BF16)
    pair = (kept + swap_core(given).astype(F32)).astype(BF16)
    pair = jnp.take(pair, (zl + jnp.arange(ZL)) % ZL, axis=0)
    total = pair[0].astype(F32)
    for s in NEAR:
        total = total + lax.ppermute(pair[s], REL, near_step(s)).astype(F32)
    total = exchange(total.astype(BF16), "zh")
    own_sum = jnp.sum(total.astype(F32), axis=0).astype(BF16)

    dwide = jnp.concatenate([m * dquery for m in masks], axis=-1)
    mats4 = mats.reshape(own, per_owner, feats, feats)
    dhead = jnp.einsum(
        "onwf,owif->oni",
        dwide.reshape(own, REPS * cap, per_owner, feats),
        mats4,
        preferred_element_type=F32,
    ).astype(BF16)
    grads = jnp.concatenate([by_source(dhead), by_source(dtail)], axis=1)
    ent_part = jnp.einsum("sen,snf->sef", hot, grads, preferred_element_type=F32).astype(BF16)
    back = exchange(
        jnp.concatenate([ent_part, dpool.reshape(REPS, pool_rows // REPS, feats)], axis=1), REP
    )
    back = jnp.sum(back.astype(F32), axis=0)
    ent_grad = back[:ent_rows].astype(BF16)
    pool_own = back[ent_rows:].astype(BF16)

    all_rows = spread(own_sum, REP, REPS).reshape(rels, rows_dev, feats)
    core_grad = jnp.einsum(
        "qk,qab->akb", ordered, all_rows, preferred_element_type=F32
    ).astype(BF16)

    own_rel = jnp.einsum("wab,akb->wk", own_sum, core, preferred_element_type=F32).astype(BF16)
    small = jnp.concatenate(
        [pool_own, jnp.pad(own_rel.reshape(1, feats), ((0, 15), (0, 0)))], axis=0
    )
    small = jnp.sum(spread(small, LINE, Z).astype(F32), axis=0)
    small = (small + swap_core(small)).astype(BF16)
    small = spread(small, REP, REPS)
    pool_grad = small[:, : pool_rows // REPS].reshape(pool_rows, feats)
    rel_ordered = small[:, pool_rows // REPS].reshape(rels, feats_rel)
    rel_grad = lax.dot_general(
        order_sel, rel_ordered, (((0,), (0,)), ((), ())), preferred_element_type=F32
    )
    return (core_grad, rel_grad, ent_grad, pool_grad)


def solution(mesh):
    cut = Mesh(mesh.devices.reshape(ZH, ZL, CORES, 4, 4), REL + REP)
    whole = REL + REP
    return jax.shard_map(
        body,
        mesh=cut,
        in_specs=(
            P(REL, None, None),
            P(),
            P(whole, None),
            P(),
            P(),
            P(whole),
            P(whole),
            P(whole),
            P(whole, None),
        ),
        out_specs=(P(REL, None, None), P(), P(whole, None), P()),
        check_vma=False,
    )
```

```python
import jax
import jax.numpy as jnp
from jax import lax
from jax.sharding import Mesh, PartitionSpec as P

ZH, ZL, CORES, REPS = 4, 4, 2, 16
Z = ZH * ZL
REL = ("zh", "zl", "core")
REP = ("y", "x")
LINE = ("zh", "zl")
STEPS = (0, 1, 2, 3)
EXTRA = 16
F32 = jnp.float32
BF16 = jnp.bfloat16


def order_tables(owner_of, per_owner):
    count = owner_of.shape[0]
    index = jnp.arange(count, dtype=jnp.int32)
    same = owner_of[:, None] == owner_of[None, :]
    rank = jnp.sum((same & (index[None, :] < index[:, None])).astype(jnp.int32), axis=1)
    return (rank, owner_of * per_owner + rank)


def exchange(blocks, axis):
    return lax.all_to_all(blocks, axis, split_axis=0, concat_axis=0, tiled=True)


def spread(block, axis, count):
    return exchange(jnp.broadcast_to(block[None], (count,) + block.shape), axis)


def near_by(step, core):
    return jnp.where(step == 2, 2 - 4 * core, jnp.where(step == 3, -1, step))


def near_move(block, step):
    pairs = []
    for z in range(Z):
        for core in range(CORES):
            by = (0, 1, 2 - 4 * core, -1)[step]
            pairs.append((z * CORES + core, (z + by) % Z * CORES + core))
    return lax.ppermute(block, REL, pairs)


def far_move(block, step):
    return lax.ppermute(block, LINE, [(z, (z + 4 * step) % Z) for z in range(Z)])


def swap_core(block):
    return lax.ppermute(block, "core", [(0, 1), (1, 0)])


def body(core, rel_emb, ents, pool, owner_of, rel_ids, head_ids, tail_ids, fill):
    rels, feats_rel = rel_emb.shape
    rows_dev, _, feats = core.shape
    owners = fill.shape[1]
    cap = rel_ids.shape[0] // owners
    per_owner = rels // owners
    own = owners // REPS
    mine = own * per_owner
    seats = own * cap
    ent_rows = ents.shape[0]
    pool_rows = pool.shape[0]
    pool_dev = pool_rows // (Z * CORES)
    scale = 1.0 / REPS
    g = lax.axis_index(REP)
    z = lax.axis_index(LINE)
    c = lax.axis_index("core")

    rank, slot_of = order_tables(owner_of, per_owner)
    qindex = jnp.arange(rels, dtype=jnp.int32)
    order_sel = (slot_of[None, :] == qindex[:, None]).astype(BF16)
    ordered = jnp.dot(order_sel, rel_emb, preferred_element_type=F32).astype(BF16)

    own_rows = lax.dynamic_slice_in_dim(ordered, g * mine, mine, 0)
    part = jnp.einsum("wk,akb->wab", own_rows, core, preferred_element_type=F32).astype(BF16)
    far = jnp.stack([part] + [far_move(part, p) for p in STEPS[1:]])
    half = jnp.stack([far] + [near_move(far, s) for s in STEPS[1:]])
    half = half.reshape(Z, mine, rows_dev, feats)
    other = swap_core(half)
    line_z = jnp.arange(Z, dtype=jnp.int32)

    def in_order(blocks, core_of):
        s = (z - line_z) % 4
        p = ((z - near_by(s, core_of) - line_z) % Z) // 4
        return jnp.take(blocks, s * 4 + p, axis=0)

    half, other = in_order(half, c), in_order(other, 1 - c)
    both = jnp.where(c == 0, jnp.stack([half, other]), jnp.stack([other, half]))
    mats = jnp.transpose(both, (2, 1, 0, 3, 4)).reshape(own, per_owner * feats, feats)

    relhot = rel_ids[None, :] == jnp.arange(rels, dtype=jnp.int32)[:, None]
    rank_slot = jnp.sum(jnp.where(relhot, rank[:, None], 0), axis=0)
    used = (jnp.arange(cap, dtype=jnp.int32)[None, :] < fill[0][:, None]).astype(jnp.int32)
    numbers = jnp.concatenate(
        [a.reshape(REPS, seats) for a in (head_ids, tail_ids, rank_slot, used)], axis=1
    ).astype(BF16)
    numbers = jnp.pad(numbers[:, None, :], ((0, 0), (0, EXTRA - 1), (0, feats - 4 * seats)))
    sent = jnp.concatenate(
        [jnp.broadcast_to(ents[None], (REPS, ent_rows, feats)), numbers], axis=1
    )
    got = exchange(sent, REP)
    table = got[:, :ent_rows]
    line = got[:, ent_rows].astype(jnp.int32)
    hot = (
        line[:, None, : 2 * seats] == jnp.arange(ent_rows, dtype=jnp.int32)[None, :, None]
    ).astype(BF16)
    rows = jnp.einsum("sen,sef->snf", hot, table, preferred_element_type=F32).astype(BF16)

    def by_owner(a):
        a = a.reshape((REPS, own, cap) + a.shape[2:])
        return jnp.swapaxes(a, 0, 1).reshape((own, REPS * cap) + a.shape[3:])

    def by_source(a):
        a = a.reshape((own, REPS, cap) + a.shape[2:])
        return jnp.swapaxes(a, 0, 1).reshape((REPS, seats) + a.shape[3:])

    heads = by_owner(rows[:, :seats])
    tails = by_owner(rows[:, seats:])
    rank_got = by_owner(line[:, 2 * seats : 3 * seats])
    live = by_owner(line[:, 3 * seats : 4 * seats]).astype(F32)
    mask = [live * (rank_got == w).astype(F32) for w in range(per_owner)]
    masks = [m[..., None].astype(BF16) for m in mask]
    heads_wide = jnp.concatenate([m * heads for m in masks], axis=-1)

    query = jnp.einsum("oni,oif->onf", heads_wide, mats, preferred_element_type=F32).astype(BF16)
    qfloat = query.astype(F32)
    positive = jnp.sum(qfloat * tails.astype(F32), axis=-1)
    negative = jnp.einsum("onf,pf->onp", query, pool, preferred_element_type=F32)
    gpos = -jax.nn.sigmoid(-positive) * live * scale
    gneg = (jax.nn.sigmoid(negative) * (live * scale / pool_rows)[..., None]).astype(BF16)
    dquery = (
        gpos[..., None] * tails.astype(F32)
        + jnp.einsum("onp,pf->onf", gneg, pool, preferred_element_type=F32)
    ).astype(BF16)
    dtail = (gpos[..., None] * qfloat).astype(BF16)
    dpool = jnp.einsum("onp,onf->pf", gneg, query, preferred_element_type=F32)
    dmats = jnp.einsum("oni,onf->oif", heads_wide, dquery, preferred_element_type=F32)

    dwide = jnp.concatenate([m * dquery for m in masks], axis=-1)
    mats4 = mats.reshape(own, per_owner, feats, feats)
    dhead = jnp.einsum(
        "onwf,owif->oni",
        dwide.reshape(own, REPS * cap, per_owner, feats),
        mats4,
        preferred_element_type=F32,
    ).astype(BF16)
    grads = jnp.concatenate([by_source(dhead), by_source(dtail)], axis=1)
    ent_part = jnp.einsum("sen,snf->sef", hot, grads, preferred_element_type=F32).astype(BF16)

    dm = dmats.reshape(mine, Z, CORES, rows_dev, feats)
    dm = jnp.transpose(dm, (2, 1, 0, 3, 4)).reshape(CORES, Z, mine * rows_dev, feats)
    dp = jnp.swapaxes(dpool.reshape(Z, CORES, pool_dev, feats), 0, 1)
    dm = jnp.concatenate([dm, dp], axis=2)
    kept = lax.dynamic_index_in_dim(dm, c, 0, keepdims=False)
    given = lax.dynamic_index_in_dim(dm, 1 - c, 0, keepdims=False).astype(BF16)
    pair = (kept + swap_core(given).astype(F32)).astype(BF16)
    steps = jnp.arange(Z, dtype=jnp.int32) // 4
    target = (z + near_by(steps, c) + 4 * (jnp.arange(Z, dtype=jnp.int32) % 4)) % Z
    pair = jnp.take(pair, target, axis=0).reshape(4, 4, mine * rows_dev + pool_dev, feats)
    pair, ent_part = lax.optimization_barrier((pair, ent_part))
    back = exchange(ent_part, REP)
    total = pair[0].astype(F32)
    for s in STEPS[1:]:
        total = total + near_move(pair[s], s).astype(F32)
    total = total.astype(BF16)
    own_sum = total[0].astype(F32)
    for p in STEPS[1:]:
        own_sum = own_sum + far_move(total[p], p).astype(F32)
    own_sum = own_sum.astype(BF16)

    own_sum, back = lax.optimization_barrier((own_sum, back))
    ent_grad = jnp.sum(back.astype(F32), axis=0).astype(BF16)
    all_sums = spread(own_sum, REP, REPS)
    all_rows = all_sums[:, : mine * rows_dev].reshape(rels, rows_dev, feats)
    pool_own = jnp.sum(all_sums[:, mine * rows_dev :].astype(F32), axis=0).astype(BF16)
    rel_own = jnp.einsum("qab,akb->qk", all_rows, core, preferred_element_type=F32).astype(BF16)

    rel_rows = rels * feats_rel // feats
    pool_z = pool_own[None]
    for axis in ("zh", "zl"):
        small = spread(
            jnp.concatenate([rel_own.reshape(rel_rows, feats), pool_z.reshape(-1, feats)]), axis, 4
        )
        rel_own = jnp.sum(small[:, :rel_rows].astype(F32), axis=0).astype(BF16)
        pool_z = small[:, rel_rows:]
    small = jnp.concatenate([rel_own, pool_z.reshape(-1, feats)])
    small_other = swap_core(small)
    rel_ordered = (small[:rel_rows].astype(F32) + small_other[:rel_rows].astype(F32)).astype(BF16)
    rel_ordered = rel_ordered.reshape(rels, feats_rel)
    halves = jnp.stack([small[rel_rows:], small_other[rel_rows:]])
    halves = jnp.where(c == 0, halves, halves[::-1]).reshape(CORES, ZL, ZH, pool_dev, feats)
    pool_grad = jnp.transpose(halves, (2, 1, 0, 3, 4)).reshape(pool_rows, feats)
    rel_grad = lax.dot_general(
        order_sel, rel_ordered, (((0,), (0,)), ((), ())), preferred_element_type=F32
    )
    core_grad = jnp.einsum(
        "qk,qab->akb", ordered, all_rows, preferred_element_type=F32
    ).astype(BF16)
    return (core_grad, rel_grad, ent_grad, pool_grad)


def solution(mesh):
    cut = Mesh(mesh.devices.reshape(ZH, ZL, CORES, 4, 4), REL + REP)
    whole = REL + REP
    return jax.shard_map(
        body,
        mesh=cut,
        in_specs=(
            P(REL, None, None),
            P(),
            P(whole, None),
            P(),
            P(),
            P(whole),
            P(whole),
            P(whole),
            P(whole, None),
        ),
        out_specs=(P(REL, None, None), P(), P(whole, None), P()),
        check_vma=False,
    )
```

```python
import functools

import jax
import jax.numpy as jnp
from jax import lax
from jax.experimental import pallas as pl
from jax.experimental.pallas import tpu as pltpu
from jax.sharding import Mesh, PartitionSpec as P

ZH, ZL, CORES, REPS = 4, 4, 2, 16
Z = ZH * ZL
REL = ("zh", "zl", "core")
REP = ("y", "x")
LINE = ("zh", "zl")
STEPS = (0, 1, 2, 3)
EXTRA = 16
F32 = jnp.float32
BF16 = jnp.bfloat16


def order_tables(owner_of, per_owner):
    count = owner_of.shape[0]
    index = jnp.arange(count, dtype=jnp.int32)
    same = owner_of[:, None] == owner_of[None, :]
    rank = jnp.sum((same & (index[None, :] < index[:, None])).astype(jnp.int32), axis=1)
    return (rank, owner_of * per_owner + rank)


def exchange(blocks, axis):
    return lax.all_to_all(blocks, axis, split_axis=0, concat_axis=0, tiled=True)


def spread(block, axis, count):
    return exchange(jnp.broadcast_to(block[None], (count,) + block.shape), axis)


def near_by(step, core):
    return jnp.where(step == 2, 2 - 4 * core, jnp.where(step == 3, -1, step))


def near_move(block, step):
    pairs = []
    for z in range(Z):
        for core in range(CORES):
            by = (0, 1, 2 - 4 * core, -1)[step]
            pairs.append((z * CORES + core, (z + by) % Z * CORES + core))
    return lax.ppermute(block, REL, pairs)


def far_move(block, step):
    return lax.ppermute(block, LINE, [(z, (z + 4 * step) % Z) for z in range(Z)])


def swap_core(block):
    return lax.ppermute(block, "core", [(0, 1), (1, 0)])


def dot(a, b, over):
    return lax.dot_general(a, b, (over, ((), ())), preferred_element_type=F32)


NN, NT, TN = ((1,), (0,)), ((1,), (1,)), ((0,), (0,))


def hot_of(line, ent_rows, columns):
    ids = line[:, : -(-columns // 128) * 128].astype(F32)[0:1, :columns]
    entity = lax.broadcasted_iota(jnp.int32, (ent_rows, columns), 0).astype(F32)
    return jnp.where(entity == ids, 1.0, 0.0).astype(BF16)


def gather_kernel(cap, got, heads, tails):
    ent_rows = got.shape[1] - EXTRA
    own = tails.shape[0]
    kinds = heads.shape[0] // own
    columns = (kinds + 1) * own * cap
    for s in range(got.shape[0]):
        hot = hot_of(got[s, ent_rows:, :], ent_rows, columns)
        rows = dot(hot, got[s, :ent_rows, :], TN).astype(BF16)
        for kind in range(kinds + 1):
            for o in range(own):
                at = (kind * own + o) * cap
                block = rows[at : at + cap]
                if kind < kinds:
                    heads[o * kinds + kind, s * cap : (s + 1) * cap, :] = block
                else:
                    tails[o, s * cap : (s + 1) * cap, :] = block


def score_kernel(scale, rows_dev, starts, heads, tails, half, other, pool, mats, dquery, dtail, given, kept, dm, dp):
    own = tails.shape[0]
    kinds = heads.shape[0] // own
    mine = heads.shape[0]
    for i in range(half.shape[0]):
        for which, source in ((0, half), (1, other)):
            at = pl.multiple_of(starts[which, i], rows_dev)
            for w in range(mine):
                mats[w, pl.ds(at, rows_dev), :] = source[i, w * rows_dev : (w + 1) * rows_dev, :]
    negatives = pool[...]
    total = None
    for o in range(own):
        query = dot(heads[o * kinds], mats[o * kinds], NN)
        for w in range(1, kinds):
            query = query + dot(heads[o * kinds + w], mats[o * kinds + w], NN)
        query = query.astype(BF16)
        qfloat = query.astype(F32)
        tail = tails[o].astype(F32)
        gpos = -jax.nn.sigmoid(-jnp.sum(qfloat * tail, axis=1, keepdims=True)) * scale
        gneg = (jax.nn.sigmoid(dot(query, negatives, NT)) * (scale / pool.shape[0])).astype(BF16)
        grad = (gpos * tail + dot(gneg, negatives, NN)).astype(BF16)
        dquery[o] = grad
        dtail[o] = (gpos * qfloat).astype(BF16)
        piece = dot(gneg, query, TN)
        total = piece if total is None else total + piece
        for w in range(kinds):
            dm[o * kinds + w] = dot(heads[o * kinds + w], grad, TN).astype(BF16)
    dp[...] = total
    pool_dev = rows_dev // 2
    for which, target in ((2, kept), (3, given)):
        for s in range(4):
            pieces = []
            for p in range(4):
                at = pl.multiple_of(starts[which, s * 4 + p], rows_dev)
                for w in range(mine):
                    row = (p * mine + w) * rows_dev
                    target[s, row : row + rows_dev, :] = dm[w, pl.ds(at, rows_dev), :]
                at = pl.multiple_of(starts[which, s * 4 + p] // 2, pool_dev)
                pieces.append(dp[pl.ds(at, pool_dev), :])
            target[s, 4 * mine * rows_dev :, :] = jnp.concatenate(pieces, axis=0).astype(BF16)


def scatter_kernel(cap, lines, dquery, dtail, mats, out, dheads):
    own = dquery.shape[0]
    kinds = mats.shape[0] // own
    columns = (kinds + 1) * own * cap
    ent_rows = out.shape[1]
    for o in range(own):
        for w in range(kinds):
            dheads[o * kinds + w] = dot(dquery[o], mats[o * kinds + w], NT).astype(BF16)
    for s in range(out.shape[0]):
        hot = hot_of(lines[s], ent_rows, columns)
        at = slice(s * cap, (s + 1) * cap)
        grads = [dheads[o * kinds + w, at, :] for w in range(kinds) for o in range(own)]
        grads += [dtail[o, at, :] for o in range(own)]
        out[s] = dot(hot, jnp.concatenate(grads, axis=0), NN).astype(BF16)


def call(kernel, outs, flops, in_specs=None, scratch=()):
    vmem = pl.BlockSpec(memory_space=pltpu.VMEM)
    return pl.pallas_call(
        kernel,
        out_shape=tuple(jax.ShapeDtypeStruct(shape, BF16) for shape in outs),
        in_specs=in_specs,
        out_specs=tuple(vmem for _ in outs),
        scratch_shapes=scratch,
        cost_estimate=pl.CostEstimate(flops=flops, bytes_accessed=1 << 23, transcendentals=0),
        compiler_params=pltpu.CompilerParams(vmem_limit_bytes=40 << 20),
    )


def body(core, rel_emb, ents, pool, owner_of, rel_ids, head_ids, tail_ids, fill):
    rels, feats_rel = rel_emb.shape
    rows_dev, _, feats = core.shape
    owners = fill.shape[1]
    cap = rel_ids.shape[0] // owners
    per_owner = rels // owners
    own = owners // REPS
    mine = own * per_owner
    seats = own * cap
    ent_rows = ents.shape[0]
    pool_rows = pool.shape[0]
    pool_dev = pool_rows // (Z * CORES)
    scale = 1.0 / REPS
    g = lax.axis_index(REP)
    z = lax.axis_index(LINE)
    c = lax.axis_index("core")

    rank, slot_of = order_tables(owner_of, per_owner)
    qindex = jnp.arange(rels, dtype=jnp.int32)
    order_sel = (slot_of[None, :] == qindex[:, None]).astype(BF16)
    ordered = jnp.dot(order_sel, rel_emb, preferred_element_type=F32).astype(BF16)

    relhot = rel_ids[None, :] == jnp.arange(rels, dtype=jnp.int32)[:, None]
    rank_slot = jnp.sum(jnp.where(relhot, rank[:, None], 0), axis=0)
    used = (jnp.arange(cap, dtype=jnp.int32)[None, :] < fill[0][:, None]).reshape(-1)
    numbers = [jnp.where(used & (rank_slot == w), head_ids, -1) for w in range(per_owner)]
    numbers.append(jnp.where(used, tail_ids, -1))
    numbers = jnp.concatenate([a.reshape(REPS, seats) for a in numbers], axis=1).astype(BF16)
    numbers = jnp.pad(numbers[:, None, :], ((0, 0), (0, EXTRA - 1), (0, feats - numbers.shape[1])))
    sent = jnp.concatenate(
        [jnp.broadcast_to(ents[None], (REPS, ent_rows, feats)), numbers], axis=1
    )
    own_rows = lax.dynamic_slice_in_dim(ordered, g * mine, mine, 0)
    own_rows, sent = lax.optimization_barrier((own_rows, sent))
    got = exchange(sent, REP)

    part = jnp.einsum("wk,akb->wab", own_rows, core, preferred_element_type=F32).astype(BF16)
    part = part.reshape(mine * rows_dev, feats)
    far = jnp.stack([part] + [far_move(part, p) for p in STEPS[1:]])
    half = jnp.concatenate([far] + [near_move(far, s) for s in STEPS[1:]])
    other = swap_core(half)

    entry = jnp.arange(Z, dtype=jnp.int32)
    starts = []
    for sign in (-1, 1):
        for core_of in (c, 1 - c):
            chip = (z + sign * (near_by(entry // 4, core_of) + 4 * (entry % 4))) % Z
            starts.append((chip * CORES + core_of) * rows_dev)
    starts = jnp.stack(starts)

    vmem = pl.BlockSpec(memory_space=pltpu.VMEM)
    smem = pl.BlockSpec(memory_space=pltpu.SMEM)
    slots = REPS * cap
    block = slots * feats * feats * 2
    heads, tails = call(
        functools.partial(gather_kernel, cap),
        ((mine, slots, feats), (own, slots, feats)),
        REPS * 3 * seats * ent_rows * feats * 2,
        [vmem],
    )(got)
    sum_rows = 4 * (mine * rows_dev + pool_dev)
    mats, dquery, dtail, given, kept = call(
        functools.partial(score_kernel, scale, rows_dev),
        (
            (mine, feats, feats),
            (own, slots, feats),
            (own, slots, feats),
            (4, sum_rows, feats),
            (4, sum_rows, feats),
        ),
        2 * mine * block + 3 * own * block // 2,
        [smem] + [vmem] * 5,
        (pltpu.VMEM((mine, feats, feats), BF16), pltpu.VMEM((pool_rows, feats), F32)),
    )(starts, heads, tails, half, other, pool)

    pair = (kept.astype(F32) + swap_core(given).astype(F32)).astype(BF16)
    pair, dquery = lax.optimization_barrier((pair, dquery))
    (ent_part,) = call(
        functools.partial(scatter_kernel, cap),
        ((REPS, ent_rows, feats),),
        mine * block + REPS * 3 * seats * ent_rows * feats * 2,
        [vmem] * 4,
        (pltpu.VMEM((mine, slots, feats), BF16),),
    )(got[:, ent_rows:], dquery, dtail, mats)
    back = exchange(ent_part, REP)
    total = pair[0].astype(F32)
    for s in STEPS[1:]:
        total = total + near_move(pair[s], s).astype(F32)
    total = total.astype(BF16)
    split = 4 * mine * rows_dev
    blocks = [
        jnp.concatenate(
            [
                total[p * mine * rows_dev : (p + 1) * mine * rows_dev],
                total[split + p * pool_dev : split + (p + 1) * pool_dev],
            ]
        )
        for p in STEPS
    ]
    own_sum = blocks[0].astype(F32)
    for p in STEPS[1:]:
        own_sum = own_sum + far_move(blocks[p], p).astype(F32)
    own_sum = own_sum.astype(BF16)

    own_sum, back = lax.optimization_barrier((own_sum, back))
    ent_grad = jnp.sum(back.astype(F32), axis=0).astype(BF16)
    all_sums = spread(own_sum, REP, REPS)
    all_rows = all_sums[:, : mine * rows_dev].reshape(rels, rows_dev, feats)
    pool_own = jnp.sum(all_sums[:, mine * rows_dev :].astype(F32), axis=0).astype(BF16)
    rel_own = jnp.einsum("qab,akb->qk", all_rows, core, preferred_element_type=F32).astype(BF16)

    rel_rows = rels * feats_rel // feats
    small = spread(jnp.concatenate([rel_own.reshape(rel_rows, feats), pool_own]), LINE, Z)
    rel_own = jnp.sum(small[:, :rel_rows].astype(F32), axis=0).astype(BF16)
    small = jnp.concatenate([rel_own, small[:, rel_rows:].reshape(-1, feats)])
    small_other = swap_core(small)
    rel_ordered = (small[:rel_rows].astype(F32) + small_other[:rel_rows].astype(F32)).astype(BF16)
    rel_ordered = rel_ordered.reshape(rels, feats_rel)
    halves = jnp.stack([small[rel_rows:], small_other[rel_rows:]])
    halves = jnp.where(c == 0, halves, halves[::-1]).reshape(CORES, Z, pool_dev, feats)
    pool_grad = jnp.swapaxes(halves, 0, 1).reshape(pool_rows, feats)
    rel_grad = lax.dot_general(
        order_sel, rel_ordered, (((0,), (0,)), ((), ())), preferred_element_type=F32
    )
    core_grad = jnp.einsum(
        "qk,qab->akb", ordered, all_rows, preferred_element_type=F32
    ).astype(BF16)
    return (core_grad, rel_grad, ent_grad, pool_grad)


def solution(mesh):
    cut = Mesh(mesh.devices.reshape(ZH, ZL, CORES, 4, 4), REL + REP)
    whole = REL + REP
    return jax.shard_map(
        body,
        mesh=cut,
        in_specs=(
            P(REL, None, None),
            P(),
            P(whole, None),
            P(),
            P(),
            P(whole),
            P(whole),
            P(whole),
            P(whole, None),
        ),
        out_specs=(P(REL, None, None), P(), P(whole, None), P()),
        check_vma=False,
    )
```

```python
import functools

import jax
import jax.numpy as jnp
from jax import lax
from jax.experimental import pallas as pl
from jax.experimental.pallas import tpu as pltpu
from jax.sharding import Mesh, PartitionSpec as P

ZH, ZL, CORES, REPS = 4, 4, 2, 16
Z = ZH * ZL
REL = ("zh", "zl", "core")
REP = ("y", "x")
LINE = ("zh", "zl")
STEPS = (0, 1, 2, 3)
EXTRA = 16
F32 = jnp.float32
BF16 = jnp.bfloat16


def order_tables(owner_of, per_owner):
    count = owner_of.shape[0]
    index = jnp.arange(count, dtype=jnp.int32)
    same = owner_of[:, None] == owner_of[None, :]
    rank = jnp.sum((same & (index[None, :] < index[:, None])).astype(jnp.int32), axis=1)
    return (rank, owner_of * per_owner + rank)


def exchange(blocks, axis):
    return lax.all_to_all(blocks, axis, split_axis=0, concat_axis=0, tiled=True)


def spread(block, axis, count):
    return exchange(jnp.broadcast_to(block[None], (count,) + block.shape), axis)


def near_by(step, core):
    return jnp.where(step == 2, 2 - 4 * core, jnp.where(step == 3, -1, step))


def near_move(block, step):
    pairs = []
    for z in range(Z):
        for core in range(CORES):
            by = (0, 1, 2 - 4 * core, -1)[step]
            pairs.append((z * CORES + core, (z + by) % Z * CORES + core))
    return lax.ppermute(block, REL, pairs)


def far_move(block, step):
    return lax.ppermute(block, LINE, [(z, (z + 4 * step) % Z) for z in range(Z)])


def swap_core(block):
    return lax.ppermute(block, "core", [(0, 1), (1, 0)])


def dot(a, b, over):
    return lax.dot_general(a, b, (over, ((), ())), preferred_element_type=F32)


NN, NT, TN = ((1,), (0,)), ((1,), (1,)), ((0,), (0,))


def hot_of(ids, ent_rows):
    entity = lax.broadcasted_iota(jnp.int32, (ent_rows, ids.shape[1]), 0).astype(F32)
    return jnp.where(entity == ids, 1.0, 0.0).astype(BF16)


def gather_kernel(cap, names, table, ids, heads, tails):
    ent_rows = table.shape[1] - EXTRA
    own = tails.shape[0]
    kinds = heads.shape[0] // own
    seats = own * cap
    columns = (kinds + 1) * seats
    row = lax.broadcasted_iota(jnp.int32, (EXTRA, 4 * seats), 0)
    lines = []
    for s in range(table.shape[0]):
        line = table[s, ent_rows:, :].astype(F32)[:, : 4 * seats]
        lines.append(jnp.sum(jnp.where(row == names[own * kinds], line, 0.0), axis=0, keepdims=True))
    lines = jnp.concatenate(lines, axis=0)
    head, tail, relation, limit = [lines[:, i * seats : (i + 1) * seats] for i in range(4)]
    seat = lax.broadcasted_iota(jnp.int32, head.shape, 1)
    live = (seat % cap).astype(F32) < limit
    found = []
    for w in range(kinds):
        name = jnp.full(head.shape, names[w], jnp.int32)
        for o in range(1, own):
            name = jnp.where(seat >= o * cap, names[o * kinds + w], name)
        found.append(jnp.where(live & (relation == name.astype(F32)), head, -1.0))
    found.append(jnp.where(live, tail, -1.0))
    ids[...] = jnp.concatenate(found + [jnp.full(head.shape, -1.0, F32)], axis=1)
    for s in range(table.shape[0]):
        hot = hot_of(ids[s : s + 1, :columns], ent_rows)
        rows = dot(hot, table[s, :ent_rows, :], TN).astype(BF16)
        for kind in range(kinds + 1):
            for o in range(own):
                at = (kind * own + o) * cap
                block = rows[at : at + cap]
                if kind < kinds:
                    heads[o * kinds + kind, s * cap : (s + 1) * cap, :] = block
                else:
                    tails[o, s * cap : (s + 1) * cap, :] = block


def score_kernel(scale, rows_dev, starts, heads, tails, half, other, pool, mats, dquery, dtail, given, kept, dm, dp):
    own = tails.shape[0]
    kinds = heads.shape[0] // own
    mine = heads.shape[0]
    for i in range(half.shape[0]):
        for which, source in ((0, half), (1, other)):
            at = pl.multiple_of(starts[which, i], rows_dev)
            for w in range(mine):
                mats[w, pl.ds(at, rows_dev), :] = source[i, w * rows_dev : (w + 1) * rows_dev, :]
    negatives = pool[...]
    total = None
    for o in range(own):
        query = dot(heads[o * kinds], mats[o * kinds], NN)
        for w in range(1, kinds):
            query = query + dot(heads[o * kinds + w], mats[o * kinds + w], NN)
        query = query.astype(BF16)
        qfloat = query.astype(F32)
        tail = tails[o].astype(F32)
        gpos = -jax.nn.sigmoid(-jnp.sum(qfloat * tail, axis=1, keepdims=True)) * scale
        gneg = (jax.nn.sigmoid(dot(query, negatives, NT)) * (scale / pool.shape[0])).astype(BF16)
        grad = (gpos * tail + dot(gneg, negatives, NN)).astype(BF16)
        dquery[o] = grad
        dtail[o] = (gpos * qfloat).astype(BF16)
        piece = dot(gneg, query, TN)
        total = piece if total is None else total + piece
        for w in range(kinds):
            dm[o * kinds + w] = dot(heads[o * kinds + w], grad, TN).astype(BF16)
    dp[...] = total
    pool_dev = rows_dev // 2
    for which, target in ((2, kept), (3, given)):
        for s in range(4):
            pieces = []
            for p in range(4):
                at = pl.multiple_of(starts[which, s * 4 + p], rows_dev)
                for w in range(mine):
                    row = (p * mine + w) * rows_dev
                    target[s, row : row + rows_dev, :] = dm[w, pl.ds(at, rows_dev), :]
                at = pl.multiple_of(starts[which, s * 4 + p] // 2, pool_dev)
                pieces.append(dp[pl.ds(at, pool_dev), :])
            target[s, 4 * mine * rows_dev :, :] = jnp.concatenate(pieces, axis=0).astype(BF16)


def scatter_kernel(cap, ids, dquery, dtail, mats, out, dheads):
    own = dquery.shape[0]
    kinds = mats.shape[0] // own
    columns = (kinds + 1) * own * cap
    ent_rows = out.shape[1]
    for o in range(own):
        for w in range(kinds):
            dheads[o * kinds + w] = dot(dquery[o], mats[o * kinds + w], NT).astype(BF16)
    for s in range(out.shape[0]):
        hot = hot_of(ids[s : s + 1, :columns], ent_rows)
        at = slice(s * cap, (s + 1) * cap)
        grads = [dheads[o * kinds + w, at, :] for w in range(kinds) for o in range(own)]
        grads += [dtail[o, at, :] for o in range(own)]
        out[s] = dot(hot, jnp.concatenate(grads, axis=0), NN).astype(BF16)


def core_kernel(rows_dev, ordered, sums, out, wide):
    rels = ordered.shape[0]
    each = rels // sums.shape[0] * rows_dev
    lanes = wide.shape[0]
    for s in range(sums.shape[0]):
        rows = sums[s, :each, :].astype(F32)
        for lane in range(lanes):
            wide[lane, s * each : (s + 1) * each, :] = rows[:, lane * 128 : (lane + 1) * 128]
    weights = ordered[...]
    for a in range(rows_dev):
        rows = [wide[lane, pl.ds(a, rels, stride=rows_dev), :] for lane in range(lanes)]
        out[a] = dot(weights, jnp.concatenate(rows, axis=1).astype(BF16), TN).astype(BF16)


def call(kernel, outs, flops, in_specs, scratch=(), dtypes=None):
    vmem = pl.BlockSpec(memory_space=pltpu.VMEM)
    return pl.pallas_call(
        kernel,
        out_shape=tuple(
            jax.ShapeDtypeStruct(shape, dtype) for shape, dtype in zip(outs, dtypes or [BF16] * len(outs))
        ),
        in_specs=in_specs,
        out_specs=tuple(vmem for _ in outs),
        scratch_shapes=scratch,
        cost_estimate=pl.CostEstimate(flops=flops, bytes_accessed=1 << 23, transcendentals=0),
        compiler_params=pltpu.CompilerParams(vmem_limit_bytes=40 << 20),
    )


def body(core, rel_emb, ents, pool, owner_of, rel_ids, head_ids, tail_ids, fill):
    rels, feats_rel = rel_emb.shape
    rows_dev, _, feats = core.shape
    owners = fill.shape[1]
    cap = rel_ids.shape[0] // owners
    per_owner = rels // owners
    own = owners // REPS
    mine = own * per_owner
    seats = own * cap
    ent_rows = ents.shape[0]
    pool_rows = pool.shape[0]
    pool_dev = pool_rows // (Z * CORES)
    scale = 1.0 / REPS
    g = lax.axis_index(REP)
    z = lax.axis_index(LINE)
    c = lax.axis_index("core")

    rank, slot_of = order_tables(owner_of, per_owner)
    qindex = jnp.arange(rels, dtype=jnp.int32)
    order_sel = (slot_of[None, :] == qindex[:, None]).astype(BF16)
    ordered = jnp.dot(order_sel, rel_emb, preferred_element_type=F32).astype(BF16)

    limits = jnp.broadcast_to(fill[0][:, None], (owners, cap))
    numbers = [a.reshape(REPS, seats) for a in (head_ids, tail_ids, rel_ids, limits)]
    numbers = jnp.concatenate(numbers, axis=1).astype(BF16)
    numbers = jnp.pad(numbers, ((0, EXTRA - REPS), (0, feats - numbers.shape[1])))
    table = lax.all_gather(jnp.concatenate([ents, numbers]), REP, axis=0, tiled=False)

    vmem = pl.BlockSpec(memory_space=pltpu.VMEM)
    smem = pl.BlockSpec(memory_space=pltpu.SMEM)
    slots = REPS * cap
    block = slots * feats * feats * 2

    own_rows = lax.dynamic_slice_in_dim(ordered, g * mine, mine, 0)
    part = jnp.einsum("wk,akb->wab", own_rows, core, preferred_element_type=F32).astype(BF16)
    part = part.reshape(mine * rows_dev, feats)
    far = jnp.stack([part] + [far_move(part, p) for p in STEPS[1:]])
    half = jnp.concatenate([far] + [near_move(far, s) for s in STEPS[1:]])
    other = swap_core(half)

    named = slot_of[None, :] == g * mine + jnp.arange(mine, dtype=jnp.int32)[:, None]
    names = jnp.sum(jnp.where(named, qindex[None, :], 0), axis=1)
    names = jnp.concatenate([names, g[None]]).astype(jnp.int32)
    ids, heads, tails = call(
        functools.partial(gather_kernel, cap),
        ((REPS, 4 * seats), (mine, slots, feats), (own, slots, feats)),
        REPS * 3 * seats * ent_rows * feats * 2,
        [smem, vmem],
        dtypes=(F32, BF16, BF16),
    )(names, table)

    entry = jnp.arange(Z, dtype=jnp.int32)
    starts = []
    for sign in (-1, 1):
        for core_of in (c, 1 - c):
            chip = (z + sign * (near_by(entry // 4, core_of) + 4 * (entry % 4))) % Z
            starts.append((chip * CORES + core_of) * rows_dev)
    starts = jnp.stack(starts)

    split = 4 * mine * rows_dev
    sum_rows = split + 4 * pool_dev
    mats, dquery, dtail, given, kept = call(
        functools.partial(score_kernel, scale, rows_dev),
        (
            (mine, feats, feats),
            (own, slots, feats),
            (own, slots, feats),
            (4, sum_rows, feats),
            (4, sum_rows, feats),
        ),
        2 * mine * block + 3 * own * block // 2,
        [smem] + [vmem] * 5,
        (pltpu.VMEM((mine, feats, feats), BF16), pltpu.VMEM((pool_rows, feats), F32)),
    )(starts, heads, tails, half, other, pool)

    (sent,) = call(
        functools.partial(scatter_kernel, cap),
        ((REPS, ent_rows, feats),),
        mine * block + REPS * 3 * seats * ent_rows * feats * 2,
        [vmem] * 4,
        (pltpu.VMEM((mine, slots, feats), BF16),),
    )(ids, dquery, dtail, mats)

    given, sent = lax.optimization_barrier((swap_core(given), sent))
    back = exchange(sent, REP)
    pair = (kept.astype(F32) + given.astype(F32)).astype(BF16)
    total = pair[0].astype(F32)
    for s in STEPS[1:]:
        total = total + near_move(pair[s], s).astype(F32)
    total = total.astype(BF16)
    each = mine * rows_dev
    blocks = [
        jnp.concatenate(
            [
                total[p * each : (p + 1) * each],
                total[split + p * pool_dev : split + (p + 1) * pool_dev],
            ]
        )
        for p in STEPS
    ]
    own_sum = blocks[0].astype(F32)
    for p in STEPS[1:]:
        own_sum = own_sum + far_move(blocks[p], p).astype(F32)
    own_sum, back = lax.optimization_barrier((own_sum.astype(BF16), back))
    ent_grad = jnp.sum(back.astype(F32), axis=0).astype(BF16)

    sums = spread(own_sum, REP, REPS)
    rel_own = jnp.einsum(
        "gwab,akb->gwk",
        sums[:, :each].reshape(REPS, mine, rows_dev, feats),
        core,
        preferred_element_type=F32,
    ).astype(BF16)
    pool_own = jnp.sum(sums[:, each:].astype(F32), axis=0).astype(BF16)

    rel_rows = rels * feats_rel // feats
    small = spread(jnp.concatenate([rel_own.reshape(rel_rows, feats), pool_own]), LINE, Z)
    (core_grad,) = call(
        functools.partial(core_kernel, rows_dev),
        ((rows_dev, feats_rel, feats),),
        2 * rows_dev * feats_rel * rels * feats,
        [vmem] * 2,
        (pltpu.VMEM((feats // 128, rels * rows_dev, 128), F32),),
    )(ordered, sums)
    small, core_grad = lax.optimization_barrier((small, core_grad))
    rel_own = jnp.sum(small[:, :rel_rows].astype(F32), axis=0).astype(BF16)
    small = jnp.concatenate([rel_own, small[:, rel_rows:].reshape(-1, feats)])
    small_other = swap_core(small)
    rel_ordered = (small[:rel_rows].astype(F32) + small_other[:rel_rows].astype(F32)).astype(BF16)
    rel_ordered = rel_ordered.reshape(rels, feats_rel)
    halves = jnp.stack([small[rel_rows:], small_other[rel_rows:]])
    halves = jnp.where(c == 0, halves, halves[::-1]).reshape(CORES, Z, pool_dev, feats)
    pool_grad = jnp.swapaxes(halves, 0, 1).reshape(pool_rows, feats)
    rel_grad = lax.dot_general(
        order_sel, rel_ordered, (((0,), (0,)), ((), ())), preferred_element_type=F32
    )
    return (core_grad, rel_grad, ent_grad, pool_grad)


def solution(mesh):
    cut = Mesh(mesh.devices.reshape(ZH, ZL, CORES, 4, 4), REL + REP)
    whole = REL + REP
    return jax.shard_map(
        body,
        mesh=cut,
        in_specs=(
            P(REL, None, None),
            P(),
            P(whole, None),
            P(),
            P(),
            P(whole),
            P(whole),
            P(whole),
            P(whole, None),
        ),
        out_specs=(P(REL, None, None), P(), P(whole, None), P()),
        check_vma=False,
    )
```

```python
import functools

import jax
import jax.numpy as jnp
from jax import lax
from jax.experimental import pallas as pl
from jax.experimental.pallas import tpu as pltpu
from jax.sharding import Mesh, PartitionSpec as P

ZH, ZL, CORES, REPS = 4, 4, 2, 16
Z = ZH * ZL
REL = ("zh", "zl", "core")
REP = ("y", "x")
LINE = ("zh", "zl")
STEPS = (0, 1, 2, 3)
EXTRA = 16
F32 = jnp.float32
BF16 = jnp.bfloat16


def exchange(blocks, axis):
    return lax.all_to_all(blocks, axis, split_axis=0, concat_axis=0, tiled=True)


def spread(block, axis, count):
    return exchange(jnp.broadcast_to(block[None], (count,) + block.shape), axis)


def near_by(step, core):
    return jnp.where(step == 2, 2 - 4 * core, jnp.where(step == 3, -1, step))


def near_move(block, step):
    pairs = []
    for z in range(Z):
        for core in range(CORES):
            by = (0, 1, 2 - 4 * core, -1)[step]
            pairs.append((z * CORES + core, (z + by) % Z * CORES + core))
    return lax.ppermute(block, REL, pairs)


def far_move(block, step):
    return lax.ppermute(block, LINE, [(z, (z + 4 * step) % Z) for z in range(Z)])


def swap_core(block):
    return lax.ppermute(block, "core", [(0, 1), (1, 0)])


def dot(a, b, over):
    return lax.dot_general(a, b, (over, ((), ())), preferred_element_type=F32)


NN, NT, TN = ((1,), (0,)), ((1,), (1,)), ((0,), (0,))


def order_kernel(per_owner, mine, where, owners, rel_emb, core, part, ordered, order_sel, slot_of, wide):
    owner = owners[...].astype(F32)
    rels = owner.shape[1]
    rows_dev = core.shape[0]
    count = rels // per_owner
    has = jnp.where(lax.broadcasted_iota(jnp.int32, (count, rels), 0).astype(F32) == owner, 1.0, 0.0).astype(BF16)
    same = dot(has, has, TN)
    index = lax.broadcasted_iota(jnp.int32, (rels, rels), 0)
    before = index < lax.broadcasted_iota(jnp.int32, (rels, rels), 1)
    rank = jnp.sum(jnp.where(before, same, 0.0), axis=0, keepdims=True)
    slot = owner * per_owner + rank
    slot_of[...] = slot
    chosen = jnp.where(index.astype(F32) == slot, 1.0, 0.0).astype(BF16)
    order_sel[...] = chosen
    ordered[...] = dot(chosen, rel_emb[...], NN).astype(BF16)
    first = (where[0] * mine + lax.broadcasted_iota(jnp.int32, (8, rels), 0)).astype(F32)
    own = dot(jnp.where(first == slot, 1.0, 0.0).astype(BF16), rel_emb[...], NN).astype(BF16)
    for a in range(rows_dev):
        rows = dot(own, core[a], NN)
        for w in range(mine):
            wide[w * rows_dev + a : w * rows_dev + a + 1, :] = rows[w : w + 1]
    part[...] = wide[...].astype(BF16)


def send_kernel(cap, fill, head_ids, tail_ids, rel_ids, ents, out):
    ent_rows = ents.shape[0]
    lane = lax.broadcasted_iota(jnp.int32, (1, 128), 1)
    limits = []
    for row in range(8):
        limit = jnp.full((1, 128), fill[0, row * 128 // cap], jnp.int32)
        for at in range(cap, 128, cap):
            limit = jnp.where(lane >= at, fill[0, (row * 128 + at) // cap], limit)
        limits.append(limit)
    numbers = [head_ids[...], tail_ids[...], rel_ids[...], jnp.concatenate(limits, axis=0)]
    numbers = jnp.concatenate([a.astype(F32) for a in numbers], axis=1)
    numbers = jnp.concatenate([numbers, jnp.zeros_like(numbers)], axis=0).astype(BF16)
    for s in range(out.shape[0]):
        out[s, :ent_rows, :] = ents[...]
        out[s, ent_rows:, :] = numbers


def hot_of(ids, ent_rows):
    entity = lax.broadcasted_iota(jnp.int32, (ent_rows, ids.shape[1]), 0).astype(F32)
    return jnp.where(entity == ids, 1.0, 0.0).astype(BF16)


def gather_kernel(cap, where, slot_of, table, ids, heads, tails):
    ent_rows = table.shape[1] - EXTRA
    own = tails.shape[0]
    kinds = heads.shape[0] // own
    seats = own * cap
    columns = (kinds + 1) * seats
    g = where[0]
    row = lax.broadcasted_iota(jnp.int32, (EXTRA, 512), 0)
    lines = []
    for s in range(table.shape[0]):
        line = table[s, ent_rows:, :].astype(F32)
        lines.append(jnp.sum(jnp.where(row == g * seats // 128, line, 0.0), axis=0, keepdims=True))
    lines = jnp.concatenate(lines, axis=0)
    lines = [lines[:, i * 128 : (i + 1) * 128] for i in range(4)]
    head, tail, relation, limit = [
        jnp.where(g * seats % 128 == 0, line[:, :seats], line[:, 128 - seats :]) for line in lines
    ]
    seat = lax.broadcasted_iota(jnp.int32, head.shape, 1)
    live = (seat % cap).astype(F32) < limit
    slot = slot_of[...]
    relations = lax.broadcasted_iota(jnp.int32, slot.shape, 1).astype(F32)
    found = []
    for w in range(kinds):
        name = None
        for o in range(own):
            mine = (g * own * kinds + o * kinds + w).astype(F32)
            this = jnp.sum(jnp.where(slot == mine, relations, 0.0), axis=1, keepdims=True)
            this = jnp.broadcast_to(this, head.shape)
            name = this if name is None else jnp.where(seat >= o * cap, this, name)
        found.append(jnp.where(live & (relation == name), head, -1.0))
    found.append(jnp.where(live, tail, -1.0))
    ids[...] = jnp.concatenate(found + [jnp.full(head.shape, -1.0, F32)], axis=1)
    for s in range(table.shape[0]):
        hot = hot_of(ids[s : s + 1, :columns], ent_rows)
        rows = dot(hot, table[s, :ent_rows, :], TN).astype(BF16)
        for kind in range(kinds + 1):
            for o in range(own):
                at = (kind * own + o) * cap
                block = rows[at : at + cap]
                if kind < kinds:
                    heads[o * kinds + kind, s * cap : (s + 1) * cap, :] = block
                else:
                    tails[o, s * cap : (s + 1) * cap, :] = block


def score_kernel(scale, rows_dev, starts, heads, tails, half, other, pool, mats, dquery, dtail, given, kept, dm, dp):
    own = tails.shape[0]
    kinds = heads.shape[0] // own
    mine = heads.shape[0]
    for i in range(half.shape[0]):
        for which, source in ((0, half), (1, other)):
            at = pl.multiple_of(starts[which, i], rows_dev)
            for w in range(mine):
                mats[w, pl.ds(at, rows_dev), :] = source[i, w * rows_dev : (w + 1) * rows_dev, :]
    negatives = pool[...]
    total = None
    for o in range(own):
        query = dot(heads[o * kinds], mats[o * kinds], NN)
        for w in range(1, kinds):
            query = query + dot(heads[o * kinds + w], mats[o * kinds + w], NN)
        query = query.astype(BF16)
        qfloat = query.astype(F32)
        tail = tails[o].astype(F32)
        gpos = -jax.nn.sigmoid(-jnp.sum(qfloat * tail, axis=1, keepdims=True)) * scale
        gneg = (jax.nn.sigmoid(dot(query, negatives, NT)) * (scale / pool.shape[0])).astype(BF16)
        grad = (gpos * tail + dot(gneg, negatives, NN)).astype(BF16)
        dquery[o] = grad
        dtail[o] = (gpos * qfloat).astype(BF16)
        piece = dot(gneg, query, TN)
        total = piece if total is None else total + piece
        for w in range(kinds):
            dm[o * kinds + w] = dot(heads[o * kinds + w], grad, TN).astype(BF16)
    dp[...] = total
    pool_dev = rows_dev // 2
    for which, target in ((2, kept), (3, given)):
        for s in range(4):
            pieces = []
            for p in range(4):
                at = pl.multiple_of(starts[which, s * 4 + p], rows_dev)
                for w in range(mine):
                    row = (p * mine + w) * rows_dev
                    target[s, row : row + rows_dev, :] = dm[w, pl.ds(at, rows_dev), :]
                at = pl.multiple_of(starts[which, s * 4 + p] // 2, pool_dev)
                pieces.append(dp[pl.ds(at, pool_dev), :])
            target[s, 4 * mine * rows_dev :, :] = jnp.concatenate(pieces, axis=0).astype(BF16)


def scatter_kernel(cap, ids, dquery, dtail, mats, out, dheads):
    own = dquery.shape[0]
    kinds = mats.shape[0] // own
    columns = (kinds + 1) * own * cap
    ent_rows = out.shape[1]
    for o in range(own):
        for w in range(kinds):
            dheads[o * kinds + w] = dot(dquery[o], mats[o * kinds + w], NT).astype(BF16)
    for s in range(out.shape[0]):
        hot = hot_of(ids[s : s + 1, :columns], ent_rows)
        at = slice(s * cap, (s + 1) * cap)
        grads = [dheads[o * kinds + w, at, :] for w in range(kinds) for o in range(own)]
        grads += [dtail[o, at, :] for o in range(own)]
        out[s] = dot(hot, jnp.concatenate(grads, axis=0), NN).astype(BF16)


def core_kernel(rows_dev, ordered, sums, out, wide):
    rels = ordered.shape[0]
    each = rels // sums.shape[0] * rows_dev
    lanes = wide.shape[0]
    for s in range(sums.shape[0]):
        rows = sums[s, :each, :].astype(F32)
        for lane in range(lanes):
            wide[lane, s * each : (s + 1) * each, :] = rows[:, lane * 128 : (lane + 1) * 128]
    weights = ordered[...]
    for a in range(rows_dev):
        rows = [wide[lane, pl.ds(a, rels, stride=rows_dev), :] for lane in range(lanes)]
        out[a] = dot(weights, jnp.concatenate(rows, axis=1).astype(BF16), TN).astype(BF16)


def call(kernel, outs, flops, in_specs, scratch=(), dtypes=None):
    vmem = pl.BlockSpec(memory_space=pltpu.VMEM)
    return pl.pallas_call(
        kernel,
        out_shape=tuple(
            jax.ShapeDtypeStruct(shape, dtype) for shape, dtype in zip(outs, dtypes or [BF16] * len(outs))
        ),
        in_specs=in_specs,
        out_specs=tuple(vmem for _ in outs),
        scratch_shapes=scratch,
        cost_estimate=pl.CostEstimate(flops=flops, bytes_accessed=1 << 23, transcendentals=0),
        compiler_params=pltpu.CompilerParams(vmem_limit_bytes=40 << 20),
    )


def body(core, rel_emb, ents, pool, owner_of, rel_ids, head_ids, tail_ids, fill):
    rels, feats_rel = rel_emb.shape
    rows_dev, _, feats = core.shape
    owners = fill.shape[1]
    cap = rel_ids.shape[0] // owners
    per_owner = rels // owners
    own = owners // REPS
    mine = own * per_owner
    seats = own * cap
    ent_rows = ents.shape[0]
    pool_rows = pool.shape[0]
    pool_dev = pool_rows // (Z * CORES)
    scale = 1.0 / REPS
    g = lax.axis_index(REP)
    z = lax.axis_index(LINE)
    c = lax.axis_index("core")

    vmem = pl.BlockSpec(memory_space=pltpu.VMEM)
    smem = pl.BlockSpec(memory_space=pltpu.SMEM)
    slots = REPS * cap
    block = slots * feats * feats * 2
    where = g[None].astype(jnp.int32)
    part, ordered, order_sel, slot_of = call(
        functools.partial(order_kernel, per_owner, mine),
        ((mine * rows_dev, feats), (rels, feats_rel), (rels, rels), (1, rels)),
        2 * 8 * core.size,
        [smem] + [vmem] * 3,
        (pltpu.VMEM((mine * rows_dev, feats), F32),),
        dtypes=(BF16, BF16, BF16, F32),
    )(where, owner_of.reshape(1, rels), rel_emb, core)

    (sent,) = call(
        functools.partial(send_kernel, cap),
        ((REPS, ent_rows + EXTRA, feats),),
        1 << 20,
        [smem] + [vmem] * 4,
    )(fill, *(a.reshape(-1, 128) for a in (head_ids, tail_ids, rel_ids)), ents)
    table = exchange(sent, REP)

    far = jnp.stack([part] + [far_move(part, p) for p in STEPS[1:]])
    half = jnp.concatenate([far] + [near_move(far, s) for s in STEPS[1:]])
    other = swap_core(half)

    ids, heads, tails = call(
        functools.partial(gather_kernel, cap),
        ((REPS, 4 * seats), (mine, slots, feats), (own, slots, feats)),
        REPS * 3 * seats * ent_rows * feats * 2,
        [smem, vmem, vmem],
        dtypes=(F32, BF16, BF16),
    )(where, slot_of, table)

    entry = jnp.arange(Z, dtype=jnp.int32)
    starts = []
    for sign in (-1, 1):
        for core_of in (c, 1 - c):
            chip = (z + sign * (near_by(entry // 4, core_of) + 4 * (entry % 4))) % Z
            starts.append((chip * CORES + core_of) * rows_dev)
    starts = jnp.stack(starts)

    split = 4 * mine * rows_dev
    sum_rows = split + 4 * pool_dev
    mats, dquery, dtail, given, kept = call(
        functools.partial(score_kernel, scale, rows_dev),
        (
            (mine, feats, feats),
            (own, slots, feats),
            (own, slots, feats),
            (4, sum_rows, feats),
            (4, sum_rows, feats),
        ),
        2 * mine * block + 3 * own * block // 2,
        [smem] + [vmem] * 5,
        (pltpu.VMEM((mine, feats, feats), BF16), pltpu.VMEM((pool_rows, feats), F32)),
    )(starts, heads, tails, half, other, pool)

    (sent,) = call(
        functools.partial(scatter_kernel, cap),
        ((REPS, ent_rows, feats),),
        mine * block + REPS * 3 * seats * ent_rows * feats * 2,
        [vmem] * 4,
        (pltpu.VMEM((mine, slots, feats), BF16),),
    )(ids, dquery, dtail, mats)

    given, sent = lax.optimization_barrier((swap_core(given), sent))
    back = exchange(sent, REP)
    pair = (kept.astype(F32) + given.astype(F32)).astype(BF16)
    total = pair[0].astype(F32)
    for s in STEPS[1:]:
        total = total + near_move(pair[s], s).astype(F32)
    total = total.astype(BF16)
    each = mine * rows_dev
    blocks = [
        jnp.concatenate(
            [
                total[p * each : (p + 1) * each],
                total[split + p * pool_dev : split + (p + 1) * pool_dev],
            ]
        )
        for p in STEPS
    ]
    own_sum = blocks[0].astype(F32)
    for p in STEPS[1:]:
        own_sum = own_sum + far_move(blocks[p], p).astype(F32)
    own_sum, back = lax.optimization_barrier((own_sum.astype(BF16), back))
    ent_grad = jnp.sum(back.astype(F32), axis=0).astype(BF16)

    sums = spread(own_sum, REP, REPS)
    rel_own = jnp.einsum(
        "gwab,akb->gwk",
        sums[:, :each].reshape(REPS, mine, rows_dev, feats),
        core,
        preferred_element_type=F32,
    ).astype(BF16)
    pool_own = jnp.sum(sums[:, each:].astype(F32), axis=0).astype(BF16)

    rel_rows = rels * feats_rel // feats
    small = spread(jnp.concatenate([rel_own.reshape(rel_rows, feats), pool_own]), LINE, Z)
    (core_grad,) = call(
        functools.partial(core_kernel, rows_dev),
        ((rows_dev, feats_rel, feats),),
        2 * rows_dev * feats_rel * rels * feats,
        [vmem] * 2,
        (pltpu.VMEM((feats // 128, rels * rows_dev, 128), F32),),
    )(ordered, sums)
    small, core_grad = lax.optimization_barrier((small, core_grad))
    rel_own = jnp.sum(small[:, :rel_rows].astype(F32), axis=0).astype(BF16)
    small = jnp.concatenate([rel_own, small[:, rel_rows:].reshape(-1, feats)])
    small_other = swap_core(small)
    rel_ordered = (small[:rel_rows].astype(F32) + small_other[:rel_rows].astype(F32)).astype(BF16)
    rel_ordered = rel_ordered.reshape(rels, feats_rel)
    halves = jnp.stack([small[rel_rows:], small_other[rel_rows:]])
    halves = jnp.where(c == 0, halves, halves[::-1]).reshape(CORES, Z, pool_dev, feats)
    pool_grad = jnp.swapaxes(halves, 0, 1).reshape(pool_rows, feats)
    rel_grad = lax.dot_general(
        order_sel, rel_ordered, (((0,), (0,)), ((), ())), preferred_element_type=F32
    )
    return (core_grad, rel_grad, ent_grad, pool_grad)


def solution(mesh):
    cut = Mesh(mesh.devices.reshape(ZH, ZL, CORES, 4, 4), REL + REP)
    whole = REL + REP
    return jax.shard_map(
        body,
        mesh=cut,
        in_specs=(
            P(REL, None, None),
            P(),
            P(whole, None),
            P(),
            P(),
            P(whole),
            P(whole),
            P(whole),
            P(whole, None),
        ),
        out_specs=(P(REL, None, None), P(), P(whole, None), P()),
        check_vma=False,
    )
```

```python
import functools

import jax
import jax.numpy as jnp
from jax import lax
from jax.experimental import pallas as pl
from jax.experimental.pallas import tpu as pltpu
from jax.sharding import Mesh, PartitionSpec as P

ZH, ZL, CORES, REPS = 4, 4, 2, 16
Z = ZH * ZL
REL = ("zh", "zl", "core")
REP = ("y", "x")
LINE = ("zh", "zl")
STEPS = (0, 1, 2, 3)
EXTRA = 16
F32 = jnp.float32
BF16 = jnp.bfloat16


def exchange(blocks, axis):
    return lax.all_to_all(blocks, axis, split_axis=0, concat_axis=0, tiled=True)


def spread(block, axis, count):
    return exchange(jnp.broadcast_to(block[None], (count,) + block.shape), axis)


def near_by(step, core):
    return jnp.where(step == 2, 2 - 4 * core, jnp.where(step == 3, -1, step))


def near_move(block, step):
    pairs = []
    for z in range(Z):
        for core in range(CORES):
            by = (0, 1, 2 - 4 * core, -1)[step]
            pairs.append((z * CORES + core, (z + by) % Z * CORES + core))
    return lax.ppermute(block, REL, pairs)


def far_move(block, step):
    return lax.ppermute(block, LINE, [(z, (z + 4 * step) % Z) for z in range(Z)])


def swap_core(block):
    return lax.ppermute(block, "core", [(0, 1), (1, 0)])


def dot(a, b, over):
    return lax.dot_general(a, b, (over, ((), ())), preferred_element_type=F32)


NN, NT, TN = ((1,), (0,)), ((1,), (1,)), ((0,), (0,))


def order_kernel(per_owner, mine, where, owners, rel_emb, core, part, ordered, order_sel, slot_of, own, wide):
    step = pl.program_id(0)
    rels = owners.shape[1]
    block = core.shape[0]
    rows_dev = wide.shape[0] // mine

    @pl.when(step == 0)
    def _():
        owner = owners[...].astype(F32)
        count = rels // per_owner
        has = lax.broadcasted_iota(jnp.int32, (count, rels), 0).astype(F32) == owner
        has = jnp.where(has, 1.0, 0.0).astype(BF16)
        same = dot(has, has, TN)
        index = lax.broadcasted_iota(jnp.int32, (rels, rels), 0)
        before = index < lax.broadcasted_iota(jnp.int32, (rels, rels), 1)
        rank = jnp.sum(jnp.where(before, same, 0.0), axis=0, keepdims=True)
        slot = owner * per_owner + rank
        slot_of[...] = slot
        chosen = jnp.where(index.astype(F32) == slot, 1.0, 0.0).astype(BF16)
        quarter = lax.broadcasted_iota(jnp.int32, (rels // 4, rels), 0)
        for i in range(4):
            order_sel[i] = jnp.where((quarter * 4 + i).astype(F32) == slot, 1.0, 0.0).astype(BF16)
        ordered[...] = dot(chosen, rel_emb[...], NN).astype(BF16)
        first = (where[0] * mine + lax.broadcasted_iota(jnp.int32, own.shape[:1] + (rels,), 0)).astype(F32)
        own[...] = dot(jnp.where(first == slot, 1.0, 0.0).astype(BF16), rel_emb[...], NN).astype(BF16)

    for a in range(block):
        rows = dot(own[...], core[a], NN)
        for w in range(mine):
            wide[pl.ds(w * rows_dev + step * block + a, 1), :] = rows[w : w + 1]

    @pl.when(step == pl.num_programs(0) - 1)
    def _():
        part[...] = wide[...].astype(BF16)


def send_kernel(cap, fill, head_ids, tail_ids, rel_ids, ents, out):
    ent_rows = ents.shape[0]
    lane = lax.broadcasted_iota(jnp.int32, (1, 128), 1)
    limits = []
    for row in range(8):
        limit = jnp.full((1, 128), fill[0, row * 128 // cap], jnp.int32)
        for at in range(cap, 128, cap):
            limit = jnp.where(lane >= at, fill[0, (row * 128 + at) // cap], limit)
        limits.append(limit)
    numbers = [head_ids[...], tail_ids[...], rel_ids[...], jnp.concatenate(limits, axis=0)]
    numbers = jnp.concatenate([a.astype(F32) for a in numbers], axis=1)
    numbers = jnp.concatenate([numbers, jnp.zeros_like(numbers)], axis=0).astype(BF16)
    for s in range(out.shape[0]):
        out[s, :ent_rows, :] = ents[...]
        out[s, ent_rows:, :] = numbers


def hot_of(ids, ent_rows):
    entity = lax.broadcasted_iota(jnp.int32, (ent_rows, ids.shape[1]), 0).astype(F32)
    return jnp.where(entity == ids, 1.0, 0.0).astype(BF16)


def gather_kernel(cap, where, slot_of, table, ids, heads, tails):
    ent_rows = table.shape[1] - EXTRA
    own = tails.shape[0]
    kinds = heads.shape[0] // own
    seats = own * cap
    columns = (kinds + 1) * seats
    g = where[0]
    row = lax.broadcasted_iota(jnp.int32, (EXTRA, 512), 0)
    lines = []
    for s in range(table.shape[0]):
        line = table[s, ent_rows:, :].astype(F32)
        lines.append(jnp.sum(jnp.where(row == g * seats // 128, line, 0.0), axis=0, keepdims=True))
    lines = jnp.concatenate(lines, axis=0)
    lines = [lines[:, i * 128 : (i + 1) * 128] for i in range(4)]
    head, tail, relation, limit = [
        jnp.where(g * seats % 128 == 0, line[:, :seats], line[:, 128 - seats :]) for line in lines
    ]
    seat = lax.broadcasted_iota(jnp.int32, head.shape, 1)
    live = (seat % cap).astype(F32) < limit
    slot = slot_of[...]
    relations = lax.broadcasted_iota(jnp.int32, slot.shape, 1).astype(F32)
    found = []
    for w in range(kinds):
        name = None
        for o in range(own):
            mine = (g * own * kinds + o * kinds + w).astype(F32)
            this = jnp.sum(jnp.where(slot == mine, relations, 0.0), axis=1, keepdims=True)
            this = jnp.broadcast_to(this, head.shape)
            name = this if name is None else jnp.where(seat >= o * cap, this, name)
        found.append(jnp.where(live & (relation == name), head, -1.0))
    found.append(jnp.where(live, tail, -1.0))
    ids[...] = jnp.concatenate(found + [jnp.full(head.shape, -1.0, F32)], axis=1)
    for s in range(table.shape[0]):
        hot = hot_of(ids[s : s + 1, :columns], ent_rows)
        rows = dot(hot, table[s, :ent_rows, :], TN).astype(BF16)
        for kind in range(kinds + 1):
            for o in range(own):
                at = (kind * own + o) * cap
                block = rows[at : at + cap]
                if kind < kinds:
                    heads[o * kinds + kind, s * cap : (s + 1) * cap, :] = block
                else:
                    tails[o, s * cap : (s + 1) * cap, :] = block


def score_kernel(scale, rows_dev, starts, heads, tails, half, other, pool, mats, dquery, dtail, given, kept, dm, dp):
    own = tails.shape[0]
    kinds = heads.shape[0] // own
    mine = heads.shape[0]
    for i in range(half.shape[0]):
        for which, source in ((0, half), (1, other)):
            at = pl.multiple_of(starts[which, i], rows_dev)
            for w in range(mine):
                mats[w, pl.ds(at, rows_dev), :] = source[i, w * rows_dev : (w + 1) * rows_dev, :]
    negatives = pool[...]
    total = None
    for o in range(own):
        query = dot(heads[o * kinds], mats[o * kinds], NN)
        for w in range(1, kinds):
            query = query + dot(heads[o * kinds + w], mats[o * kinds + w], NN)
        query = query.astype(BF16)
        qfloat = query.astype(F32)
        tail = tails[o].astype(F32)
        gpos = -jax.nn.sigmoid(-jnp.sum(qfloat * tail, axis=1, keepdims=True)) * scale
        gneg = (jax.nn.sigmoid(dot(query, negatives, NT)) * (scale / pool.shape[0])).astype(BF16)
        grad = (gpos * tail + dot(gneg, negatives, NN)).astype(BF16)
        dquery[o] = grad
        dtail[o] = (gpos * qfloat).astype(BF16)
        piece = dot(gneg, query, TN)
        total = piece if total is None else total + piece
        for w in range(kinds):
            dm[o * kinds + w] = dot(heads[o * kinds + w], grad, TN).astype(BF16)
    dp[...] = total
    pool_dev = rows_dev // 2
    for which, target in ((2, kept), (3, given)):
        for s in range(4):
            pieces = []
            for p in range(4):
                at = pl.multiple_of(starts[which, s * 4 + p], rows_dev)
                for w in range(mine):
                    row = (p * mine + w) * rows_dev
                    target[s, row : row + rows_dev, :] = dm[w, pl.ds(at, rows_dev), :]
                at = pl.multiple_of(starts[which, s * 4 + p] // 2, pool_dev)
                pieces.append(dp[pl.ds(at, pool_dev), :])
            target[s, 4 * mine * rows_dev :, :] = jnp.concatenate(pieces, axis=0).astype(BF16)


def scatter_kernel(cap, ids, dquery, dtail, mats, out, dheads):
    own = dquery.shape[0]
    kinds = mats.shape[0] // own
    columns = (kinds + 1) * own * cap
    ent_rows = out.shape[1]
    for o in range(own):
        for w in range(kinds):
            dheads[o * kinds + w] = dot(dquery[o], mats[o * kinds + w], NT).astype(BF16)
    for s in range(out.shape[0]):
        hot = hot_of(ids[s : s + 1, :columns], ent_rows)
        at = slice(s * cap, (s + 1) * cap)
        grads = [dheads[o * kinds + w, at, :] for w in range(kinds) for o in range(own)]
        grads += [dtail[o, at, :] for o in range(own)]
        out[s] = dot(hot, jnp.concatenate(grads, axis=0), NN).astype(BF16)


def core_kernel(rows_dev, ordered, sums, out, wide):
    rels = ordered.shape[0]
    each = rels // sums.shape[0] * rows_dev
    lanes = wide.shape[0]
    for s in range(sums.shape[0]):
        rows = sums[s, :each, :].astype(F32)
        for lane in range(lanes):
            wide[lane, s * each : (s + 1) * each, :] = rows[:, lane * 128 : (lane + 1) * 128]
    weights = ordered[...]
    for a in range(rows_dev):
        rows = [wide[lane, pl.ds(a, rels, stride=rows_dev), :] for lane in range(lanes)]
        out[a] = dot(weights, jnp.concatenate(rows, axis=1).astype(BF16), TN).astype(BF16)


def last_kernel(where, own, other, order_sel, rel_grad, pool_grad):
    rel_rows = order_sel.shape[1]
    pool_dev = own.shape[1] - rel_rows
    first = where[1] == 0
    total = None
    for s in range(own.shape[0]):
        mine, theirs = own[s].astype(F32), other[s].astype(F32)
        both = mine[:rel_rows] + theirs[:rel_rows]
        total = both if total is None else total + both
        mine, theirs = mine[rel_rows:], theirs[rel_rows:]
        rows = [jnp.where(first, mine, theirs), jnp.where(first, theirs, mine)]
        at = 2 * pool_dev * s
        pool_grad[at : at + 2 * pool_dev, :] = jnp.concatenate(rows, axis=0).astype(BF16)
    total = total.astype(BF16)
    grad = None
    for i in range(4):
        piece = dot(order_sel[i], total[:, i * 128 : (i + 1) * 128], TN)
        grad = piece if grad is None else grad + piece
    rel_grad[...] = grad


def call(kernel, outs, flops, in_specs, scratch=(), dtypes=None):
    vmem = pl.BlockSpec(memory_space=pltpu.VMEM)
    return pl.pallas_call(
        kernel,
        out_shape=tuple(
            jax.ShapeDtypeStruct(shape, dtype) for shape, dtype in zip(outs, dtypes or [BF16] * len(outs))
        ),
        in_specs=in_specs,
        out_specs=tuple(vmem for _ in outs),
        scratch_shapes=scratch,
        cost_estimate=pl.CostEstimate(flops=flops, bytes_accessed=1 << 23, transcendentals=0),
        compiler_params=pltpu.CompilerParams(vmem_limit_bytes=40 << 20),
    )


def body(core, rel_emb, ents, pool, owner_of, rel_ids, head_ids, tail_ids, fill):
    rels, feats_rel = rel_emb.shape
    rows_dev, _, feats = core.shape
    owners = fill.shape[1]
    cap = rel_ids.shape[0] // owners
    per_owner = rels // owners
    own = owners // REPS
    mine = own * per_owner
    seats = own * cap
    ent_rows = ents.shape[0]
    pool_rows = pool.shape[0]
    pool_dev = pool_rows // (Z * CORES)
    scale = 1.0 / REPS
    g = lax.axis_index(REP)
    z = lax.axis_index(LINE)
    c = lax.axis_index("core")

    vmem = pl.BlockSpec(memory_space=pltpu.VMEM)
    smem = pl.BlockSpec(memory_space=pltpu.SMEM)
    slots = REPS * cap
    block = slots * feats * feats * 2
    where = jnp.stack([g, c]).astype(jnp.int32)
    shapes = ((mine * rows_dev, feats), (rels, feats_rel), (4, rels // 4, rels), (1, rels))
    steps = 1
    part, ordered, order_sel, slot_of = pl.pallas_call(
        functools.partial(order_kernel, per_owner, mine),
        grid=(steps,),
        out_shape=tuple(
            jax.ShapeDtypeStruct(shape, dtype) for shape, dtype in zip(shapes, (BF16, BF16, BF16, F32))
        ),
        in_specs=[
            smem,
            pl.BlockSpec((1, rels), lambda i: (0, 0)),
            pl.BlockSpec((rels, feats_rel), lambda i: (0, 0)),
            pl.BlockSpec((rows_dev // steps, feats_rel, feats), lambda i: (i, 0, 0)),
        ],
        out_specs=tuple(pl.BlockSpec(shape, lambda i, n=len(shape): (0,) * n) for shape in shapes),
        scratch_shapes=(pltpu.VMEM((16, feats_rel), BF16), pltpu.VMEM((mine * rows_dev, feats), F32)),
        cost_estimate=pl.CostEstimate(flops=16 * 2 * core.size, bytes_accessed=1 << 21, transcendentals=0),
        compiler_params=pltpu.CompilerParams(vmem_limit_bytes=60 << 20),
    )(where, owner_of.reshape(1, rels), rel_emb, core)

    (sent,) = call(
        functools.partial(send_kernel, cap),
        ((REPS, ent_rows + EXTRA, feats),),
        1 << 20,
        [smem] + [vmem] * 4,
    )(fill, *(a.reshape(-1, 128) for a in (head_ids, tail_ids, rel_ids)), ents)
    table = exchange(sent, REP)

    far = jnp.stack([part] + [far_move(part, p) for p in STEPS[1:]])
    half = jnp.concatenate([far] + [near_move(far, s) for s in STEPS[1:]])
    other = swap_core(half)

    ids, heads, tails = call(
        functools.partial(gather_kernel, cap),
        ((REPS, 4 * seats), (mine, slots, feats), (own, slots, feats)),
        REPS * 3 * seats * ent_rows * feats * 2,
        [smem, vmem, vmem],
        dtypes=(F32, BF16, BF16),
    )(where, slot_of, table)

    entry = jnp.arange(Z, dtype=jnp.int32)
    starts = []
    for sign in (-1, 1):
        for core_of in (c, 1 - c):
            chip = (z + sign * (near_by(entry // 4, core_of) + 4 * (entry % 4))) % Z
            starts.append((chip * CORES + core_of) * rows_dev)
    starts = jnp.stack(starts)

    split = 4 * mine * rows_dev
    sum_rows = split + 4 * pool_dev
    mats, dquery, dtail, given, kept = call(
        functools.partial(score_kernel, scale, rows_dev),
        (
            (mine, feats, feats),
            (own, slots, feats),
            (own, slots, feats),
            (4, sum_rows, feats),
            (4, sum_rows, feats),
        ),
        2 * mine * block + 3 * own * block // 2,
        [smem] + [vmem] * 5,
        (pltpu.VMEM((mine, feats, feats), BF16), pltpu.VMEM((pool_rows, feats), F32)),
    )(starts, heads, tails, half, other, pool)

    (sent,) = call(
        functools.partial(scatter_kernel, cap),
        ((REPS, ent_rows, feats),),
        mine * block + REPS * 3 * seats * ent_rows * feats * 2,
        [vmem] * 4,
        (pltpu.VMEM((mine, slots, feats), BF16),),
    )(ids, dquery, dtail, mats)

    given, sent = lax.optimization_barrier((swap_core(given), sent))
    back = exchange(sent, REP)
    pair = (kept.astype(F32) + given.astype(F32)).astype(BF16)
    total = pair[0].astype(F32)
    for s in STEPS[1:]:
        total = total + near_move(pair[s], s).astype(F32)
    total = total.astype(BF16)
    each = mine * rows_dev
    blocks = [
        jnp.concatenate(
            [
                total[p * each : (p + 1) * each],
                total[split + p * pool_dev : split + (p + 1) * pool_dev],
            ]
        )
        for p in STEPS
    ]
    own_sum = blocks[0].astype(F32)
    for p in STEPS[1:]:
        own_sum = own_sum + far_move(blocks[p], p).astype(F32)
    own_sum, back = lax.optimization_barrier((own_sum.astype(BF16), back))
    ent_grad = jnp.sum(back.astype(F32), axis=0).astype(BF16)

    sums = spread(own_sum, REP, REPS)
    rel_own = jnp.einsum(
        "gwab,akb->gwk",
        sums[:, :each].reshape(REPS, mine, rows_dev, feats),
        core,
        preferred_element_type=F32,
    ).astype(BF16)
    pool_own = jnp.sum(sums[:, each:].astype(F32), axis=0).astype(BF16)

    rel_rows = rels * feats_rel // feats
    small = spread(jnp.concatenate([rel_own.reshape(rel_rows, feats), pool_own]), LINE, Z)
    (core_grad,) = call(
        functools.partial(core_kernel, rows_dev),
        ((rows_dev, feats_rel, feats),),
        2 * rows_dev * feats_rel * rels * feats,
        [vmem] * 2,
        (pltpu.VMEM((feats // 128, rels * rows_dev, 128), F32),),
    )(ordered, sums)
    small, core_grad, ent_grad = lax.optimization_barrier((small, core_grad, ent_grad))
    rel_grad, pool_grad = call(
        last_kernel,
        ((rels, feats_rel), (pool_rows, feats)),
        1 << 20,
        [smem] + [vmem] * 3,
        dtypes=(F32, BF16),
    )(where, small, swap_core(small), order_sel)
    return (core_grad, rel_grad, ent_grad, pool_grad)


def solution(mesh):
    cut = Mesh(mesh.devices.reshape(ZH, ZL, CORES, 4, 4), REL + REP)
    whole = REL + REP
    return jax.shard_map(
        body,
        mesh=cut,
        in_specs=(
            P(REL, None, None),
            P(),
            P(whole, None),
            P(),
            P(),
            P(whole),
            P(whole),
            P(whole),
            P(whole, None),
        ),
        out_specs=(P(REL, None, None), P(), P(whole, None), P()),
        check_vma=False,
    )
```

```python
import functools

import jax
import jax.numpy as jnp
from jax import lax
from jax.experimental import pallas as pl
from jax.experimental.pallas import tpu as pltpu
from jax.sharding import Mesh, PartitionSpec as P

ZH, ZL, CORES, REPS = 4, 4, 2, 16
Z = ZH * ZL
REL = ("zh", "zl", "core")
REP = ("y", "x")
LINE = ("zh", "zl")
STEPS = (0, 1, 2, 3)
EXTRA = 16
F32 = jnp.float32
BF16 = jnp.bfloat16


def exchange(blocks, axis):
    return lax.all_to_all(blocks, axis, split_axis=0, concat_axis=0, tiled=True)


def spread(block, axis, count):
    return exchange(jnp.broadcast_to(block[None], (count,) + block.shape), axis)


def near_by(step, core):
    return jnp.where(step == 2, 2 - 4 * core, jnp.where(step == 3, -1, step))


def near_move(block, step):
    pairs = []
    for z in range(Z):
        for core in range(CORES):
            by = (0, 1, 2 - 4 * core, -1)[step]
            pairs.append((z * CORES + core, (z + by) % Z * CORES + core))
    return lax.ppermute(block, REL, pairs)


def far_move(block, step):
    return lax.ppermute(block, LINE, [(z, (z + 4 * step) % Z) for z in range(Z)])


def swap_core(block):
    return lax.ppermute(block, "core", [(0, 1), (1, 0)])


def dot(a, b, over):
    return lax.dot_general(a, b, (over, ((), ())), preferred_element_type=F32)


NN, NT, TN = ((1,), (0,)), ((1,), (1,)), ((0,), (0,))


def order_kernel(per_owner, mine, owners, rel_emb, core, part, ordered, order_sel, slot_of, own, wide):
    step = pl.program_id(0)
    rels = owners.shape[1]
    block = core.shape[0]
    rows_dev = wide.shape[0] // mine

    @pl.when(step == 0)
    def _():
        owner = owners[...].astype(F32)
        count = rels // per_owner
        has = lax.broadcasted_iota(jnp.int32, (count, rels), 0).astype(F32) == owner
        has = jnp.where(has, 1.0, 0.0).astype(BF16)
        same = dot(has, has, TN)
        index = lax.broadcasted_iota(jnp.int32, (rels, rels), 0)
        before = index < lax.broadcasted_iota(jnp.int32, (rels, rels), 1)
        rank = jnp.sum(jnp.where(before, same, 0.0), axis=0, keepdims=True)
        slot = owner * per_owner + rank
        slot_of[...] = slot
        chosen = jnp.where(index.astype(F32) == slot, 1.0, 0.0).astype(BF16)
        quarter = lax.broadcasted_iota(jnp.int32, (rels // 4, rels), 0)
        for i in range(4):
            order_sel[i] = jnp.where((quarter * 4 + i).astype(F32) == slot, 1.0, 0.0).astype(BF16)
        ordered[...] = dot(chosen, rel_emb[...], NN).astype(BF16)
        first = (lax.axis_index(REP) * mine + lax.broadcasted_iota(jnp.int32, own.shape[:1] + (rels,), 0)).astype(F32)
        own[...] = dot(jnp.where(first == slot, 1.0, 0.0).astype(BF16), rel_emb[...], NN).astype(BF16)

    for a in range(block):
        rows = dot(own[...], core[a], NN)
        for w in range(mine):
            wide[pl.ds(w * rows_dev + step * block + a, 1), :] = rows[w : w + 1]

    @pl.when(step == pl.num_programs(0) - 1)
    def _():
        part[...] = wide[...].astype(BF16)


def send_kernel(cap, fill, head_ids, tail_ids, rel_ids, ents, out):
    ent_rows = ents.shape[0]
    lane = lax.broadcasted_iota(jnp.int32, (1, 128), 1)
    limits = []
    for row in range(8):
        limit = jnp.full((1, 128), fill[0, row * 128 // cap], jnp.int32)
        for at in range(cap, 128, cap):
            limit = jnp.where(lane >= at, fill[0, (row * 128 + at) // cap], limit)
        limits.append(limit)
    numbers = [head_ids[...], tail_ids[...], rel_ids[...], jnp.concatenate(limits, axis=0)]
    numbers = jnp.concatenate([a.astype(F32) for a in numbers], axis=1)
    numbers = jnp.concatenate([numbers, jnp.zeros_like(numbers)], axis=0).astype(BF16)
    for s in range(out.shape[0]):
        out[s, :ent_rows, :] = ents[...]
        out[s, ent_rows:, :] = numbers


def hot_of(ids, ent_rows):
    entity = lax.broadcasted_iota(jnp.int32, (ent_rows, ids.shape[1]), 0).astype(F32)
    return jnp.where(entity == ids, 1.0, 0.0).astype(BF16)


def gather_kernel(cap, where, slot_of, table, ids, heads, tails):
    ent_rows = table.shape[1] - EXTRA
    own = tails.shape[0]
    kinds = heads.shape[0] // own
    seats = own * cap
    columns = (kinds + 1) * seats
    g = where[0]
    row = lax.broadcasted_iota(jnp.int32, (EXTRA, 512), 0)
    lines = []
    for s in range(table.shape[0]):
        line = table[s, ent_rows:, :].astype(F32)
        lines.append(jnp.sum(jnp.where(row == g * seats // 128, line, 0.0), axis=0, keepdims=True))
    lines = jnp.concatenate(lines, axis=0)
    lines = [lines[:, i * 128 : (i + 1) * 128] for i in range(4)]
    head, tail, relation, limit = [
        jnp.where(g * seats % 128 == 0, line[:, :seats], line[:, 128 - seats :]) for line in lines
    ]
    seat = lax.broadcasted_iota(jnp.int32, head.shape, 1)
    live = (seat % cap).astype(F32) < limit
    slot = slot_of[...]
    relations = lax.broadcasted_iota(jnp.int32, slot.shape, 1).astype(F32)
    found = []
    for w in range(kinds):
        name = None
        for o in range(own):
            mine = (g * own * kinds + o * kinds + w).astype(F32)
            this = jnp.sum(jnp.where(slot == mine, relations, 0.0), axis=1, keepdims=True)
            this = jnp.broadcast_to(this, head.shape)
            name = this if name is None else jnp.where(seat >= o * cap, this, name)
        found.append(jnp.where(live & (relation == name), head, -1.0))
    found.append(jnp.where(live, tail, -1.0))
    ids[...] = jnp.concatenate(found + [jnp.full(head.shape, -1.0, F32)], axis=1)
    for s in range(table.shape[0]):
        hot = hot_of(ids[s : s + 1, :columns], ent_rows)
        rows = dot(hot, table[s, :ent_rows, :], TN).astype(BF16)
        for kind in range(kinds + 1):
            for o in range(own):
                at = (kind * own + o) * cap
                block = rows[at : at + cap]
                if kind < kinds:
                    heads[o * kinds + kind, s * cap : (s + 1) * cap, :] = block
                else:
                    tails[o, s * cap : (s + 1) * cap, :] = block


def score_kernel(scale, rows_dev, starts, heads, tails, half, other, pool, mats, dquery, dtail, given, kept, dm, dp):
    own = tails.shape[0]
    kinds = heads.shape[0] // own
    mine = heads.shape[0]
    for i in range(half.shape[0]):
        for which, source in ((0, half), (1, other)):
            at = pl.multiple_of(starts[which, i], rows_dev)
            for w in range(mine):
                mats[w, pl.ds(at, rows_dev), :] = source[i, w * rows_dev : (w + 1) * rows_dev, :]
    negatives = pool[...]
    total = None
    for o in range(own):
        query = dot(heads[o * kinds], mats[o * kinds], NN)
        for w in range(1, kinds):
            query = query + dot(heads[o * kinds + w], mats[o * kinds + w], NN)
        query = query.astype(BF16)
        qfloat = query.astype(F32)
        tail = tails[o].astype(F32)
        gpos = -jax.nn.sigmoid(-jnp.sum(qfloat * tail, axis=1, keepdims=True)) * scale
        gneg = (jax.nn.sigmoid(dot(query, negatives, NT)) * (scale / pool.shape[0])).astype(BF16)
        grad = (gpos * tail + dot(gneg, negatives, NN)).astype(BF16)
        dquery[o] = grad
        dtail[o] = (gpos * qfloat).astype(BF16)
        piece = dot(gneg, query, TN)
        total = piece if total is None else total + piece
        for w in range(kinds):
            dm[o * kinds + w] = dot(heads[o * kinds + w], grad, TN).astype(BF16)
    dp[...] = total
    pool_dev = rows_dev // 2
    for which, target in ((2, kept), (3, given)):
        for s in range(4):
            pieces = []
            for p in range(4):
                at = pl.multiple_of(starts[which, s * 4 + p], rows_dev)
                for w in range(mine):
                    row = (p * mine + w) * rows_dev
                    target[s, row : row + rows_dev, :] = dm[w, pl.ds(at, rows_dev), :]
                at = pl.multiple_of(starts[which, s * 4 + p] // 2, pool_dev)
                pieces.append(dp[pl.ds(at, pool_dev), :])
            target[s, 4 * mine * rows_dev :, :] = jnp.concatenate(pieces, axis=0).astype(BF16)


def scatter_kernel(cap, ids, dquery, dtail, mats, out, dheads):
    own = dquery.shape[0]
    kinds = mats.shape[0] // own
    columns = (kinds + 1) * own * cap
    ent_rows = out.shape[1]
    for o in range(own):
        for w in range(kinds):
            dheads[o * kinds + w] = dot(dquery[o], mats[o * kinds + w], NT).astype(BF16)
    for s in range(out.shape[0]):
        hot = hot_of(ids[s : s + 1, :columns], ent_rows)
        at = slice(s * cap, (s + 1) * cap)
        grads = [dheads[o * kinds + w, at, :] for w in range(kinds) for o in range(own)]
        grads += [dtail[o, at, :] for o in range(own)]
        out[s] = dot(hot, jnp.concatenate(grads, axis=0), NN).astype(BF16)


def core_kernel(rows_dev, ordered, sums, out, wide):
    rels = ordered.shape[0]
    each = rels // sums.shape[0] * rows_dev
    lanes = wide.shape[0]
    for s in range(sums.shape[0]):
        rows = sums[s, :each, :].astype(F32)
        for lane in range(lanes):
            wide[lane, s * each : (s + 1) * each, :] = rows[:, lane * 128 : (lane + 1) * 128]
    weights = ordered[...]
    for a in range(rows_dev):
        rows = [wide[lane, pl.ds(a, rels, stride=rows_dev), :] for lane in range(lanes)]
        out[a] = dot(weights, jnp.concatenate(rows, axis=1).astype(BF16), TN).astype(BF16)


def last_kernel(where, own, other, order_sel, rel_grad, pool_grad):
    rel_rows = order_sel.shape[1]
    pool_dev = own.shape[1] - rel_rows
    first = where[1] == 0
    total = None
    for s in range(own.shape[0]):
        mine, theirs = own[s].astype(F32), other[s].astype(F32)
        both = mine[:rel_rows] + theirs[:rel_rows]
        total = both if total is None else total + both
        mine, theirs = mine[rel_rows:], theirs[rel_rows:]
        rows = [jnp.where(first, mine, theirs), jnp.where(first, theirs, mine)]
        at = 2 * pool_dev * s
        pool_grad[at : at + 2 * pool_dev, :] = jnp.concatenate(rows, axis=0).astype(BF16)
    total = total.astype(BF16)
    grad = None
    for i in range(4):
        piece = dot(order_sel[i], total[:, i * 128 : (i + 1) * 128], TN)
        grad = piece if grad is None else grad + piece
    rel_grad[...] = grad


def call(kernel, outs, flops, in_specs, scratch=(), dtypes=None):
    vmem = pl.BlockSpec(memory_space=pltpu.VMEM)
    return pl.pallas_call(
        kernel,
        out_shape=tuple(
            jax.ShapeDtypeStruct(shape, dtype) for shape, dtype in zip(outs, dtypes or [BF16] * len(outs))
        ),
        in_specs=in_specs,
        out_specs=tuple(vmem for _ in outs),
        scratch_shapes=scratch,
        cost_estimate=pl.CostEstimate(flops=flops, bytes_accessed=1 << 23, transcendentals=0),
        compiler_params=pltpu.CompilerParams(vmem_limit_bytes=40 << 20),
    )


def body(core, rel_emb, ents, pool, owner_of, rel_ids, head_ids, tail_ids, fill):
    rels, feats_rel = rel_emb.shape
    rows_dev, _, feats = core.shape
    owners = fill.shape[1]
    cap = rel_ids.shape[0] // owners
    per_owner = rels // owners
    own = owners // REPS
    mine = own * per_owner
    seats = own * cap
    ent_rows = ents.shape[0]
    pool_rows = pool.shape[0]
    pool_dev = pool_rows // (Z * CORES)
    scale = 1.0 / REPS
    g = lax.axis_index(REP)
    z = lax.axis_index(LINE)
    c = lax.axis_index("core")

    vmem = pl.BlockSpec(memory_space=pltpu.VMEM)
    smem = pl.BlockSpec(memory_space=pltpu.SMEM)
    slots = REPS * cap
    block = slots * feats * feats * 2
    where = jnp.stack([g, c]).astype(jnp.int32)
    shapes = ((mine * rows_dev, feats), (rels, feats_rel), (4, rels // 4, rels), (1, rels))
    steps = 1
    part, ordered, order_sel, slot_of = pl.pallas_call(
        functools.partial(order_kernel, per_owner, mine),
        grid=(steps,),
        out_shape=tuple(
            jax.ShapeDtypeStruct(shape, dtype) for shape, dtype in zip(shapes, (BF16, BF16, BF16, F32))
        ),
        in_specs=[
            pl.BlockSpec((1, rels), lambda i: (0, 0)),
            pl.BlockSpec((rels, feats_rel), lambda i: (0, 0)),
            pl.BlockSpec((rows_dev // steps, feats_rel, feats), lambda i: (i, 0, 0)),
        ],
        out_specs=tuple(pl.BlockSpec(shape, lambda i, n=len(shape): (0,) * n) for shape in shapes),
        scratch_shapes=(pltpu.VMEM((16, feats_rel), BF16), pltpu.VMEM((mine * rows_dev, feats), F32)),
        cost_estimate=pl.CostEstimate(flops=16 * 2 * core.size, bytes_accessed=1 << 21, transcendentals=0),
        compiler_params=pltpu.CompilerParams(vmem_limit_bytes=60 << 20),
    )(owner_of.reshape(1, rels), rel_emb, core)

    (sent,) = call(
        functools.partial(send_kernel, cap),
        ((REPS, ent_rows + EXTRA, feats),),
        1 << 20,
        [smem] + [vmem] * 4,
    )(fill, *(a.reshape(-1, 128) for a in (head_ids, tail_ids, rel_ids)), ents)
    table = exchange(sent, REP)

    far = jnp.stack([part] + [far_move(part, p) for p in STEPS[1:]])
    half = jnp.concatenate([far] + [near_move(far, s) for s in STEPS[1:]])
    other = swap_core(half)

    ids, heads, tails = call(
        functools.partial(gather_kernel, cap),
        ((REPS, 4 * seats), (mine, slots, feats), (own, slots, feats)),
        REPS * 3 * seats * ent_rows * feats * 2,
        [smem, vmem, vmem],
        dtypes=(F32, BF16, BF16),
    )(where, slot_of, table)

    entry = jnp.arange(Z, dtype=jnp.int32)
    starts = []
    for sign in (-1, 1):
        for core_of in (c, 1 - c):
            chip = (z + sign * (near_by(entry // 4, core_of) + 4 * (entry % 4))) % Z
            starts.append((chip * CORES + core_of) * rows_dev)
    starts = jnp.stack(starts)

    split = 4 * mine * rows_dev
    sum_rows = split + 4 * pool_dev
    mats, dquery, dtail, given, kept = call(
        functools.partial(score_kernel, scale, rows_dev),
        (
            (mine, feats, feats),
            (own, slots, feats),
            (own, slots, feats),
            (4, sum_rows, feats),
            (4, sum_rows, feats),
        ),
        2 * mine * block + 3 * own * block // 2,
        [smem] + [vmem] * 5,
        (pltpu.VMEM((mine, feats, feats), BF16), pltpu.VMEM((pool_rows, feats), F32)),
    )(starts, heads, tails, half, other, pool)

    (sent,) = call(
        functools.partial(scatter_kernel, cap),
        ((REPS, ent_rows, feats),),
        mine * block + REPS * 3 * seats * ent_rows * feats * 2,
        [vmem] * 4,
        (pltpu.VMEM((mine, slots, feats), BF16),),
    )(ids, dquery, dtail, mats)

    given, sent = lax.optimization_barrier((swap_core(given), sent))
    back = exchange(sent, REP)
    pair = (kept.astype(F32) + given.astype(F32)).astype(BF16)
    total = pair[0].astype(F32)
    for s in STEPS[1:]:
        total = total + near_move(pair[s], s).astype(F32)
    total = total.astype(BF16)
    each = mine * rows_dev
    blocks = [
        jnp.concatenate(
            [
                total[p * each : (p + 1) * each],
                total[split + p * pool_dev : split + (p + 1) * pool_dev],
            ]
        )
        for p in STEPS
    ]
    own_sum = blocks[0].astype(F32)
    for p in STEPS[1:]:
        own_sum = own_sum + far_move(blocks[p], p).astype(F32)
    own_sum, back = lax.optimization_barrier((own_sum.astype(BF16), back))
    ent_grad = jnp.sum(back.astype(F32), axis=0).astype(BF16)

    sums = spread(own_sum, REP, REPS)
    rel_own = jnp.einsum(
        "gwab,akb->gwk",
        sums[:, :each].reshape(REPS, mine, rows_dev, feats),
        core,
        preferred_element_type=F32,
    ).astype(BF16)
    pool_own = jnp.sum(sums[:, each:].astype(F32), axis=0).astype(BF16)

    rel_rows = rels * feats_rel // feats
    small = spread(jnp.concatenate([rel_own.reshape(rel_rows, feats), pool_own]), LINE, Z)
    (core_grad,) = call(
        functools.partial(core_kernel, rows_dev),
        ((rows_dev, feats_rel, feats),),
        2 * rows_dev * feats_rel * rels * feats,
        [vmem] * 2,
        (pltpu.VMEM((feats // 128, rels * rows_dev, 128), F32),),
    )(ordered, sums)
    small, core_grad, ent_grad = lax.optimization_barrier((small, core_grad, ent_grad))
    rel_grad, pool_grad = call(
        last_kernel,
        ((rels, feats_rel), (pool_rows, feats)),
        1 << 20,
        [smem] + [vmem] * 3,
        dtypes=(F32, BF16),
    )(where, small, swap_core(small), order_sel)
    return (core_grad, rel_grad, ent_grad, pool_grad)


def solution(mesh):
    cut = Mesh(mesh.devices.reshape(ZH, ZL, CORES, 4, 4), REL + REP)
    whole = REL + REP
    return jax.shard_map(
        body,
        mesh=cut,
        in_specs=(
            P(REL, None, None),
            P(),
            P(whole, None),
            P(),
            P(),
            P(whole),
            P(whole),
            P(whole),
            P(whole, None),
        ),
        out_specs=(P(REL, None, None), P(), P(whole, None), P()),
        check_vma=False,
    )
```

```python
import functools

import jax
import jax.numpy as jnp
from jax import lax
from jax.experimental import pallas as pl
from jax.experimental.pallas import tpu as pltpu
from jax.sharding import Mesh, PartitionSpec as P

ZH, ZL, CORES, REPS = 4, 4, 2, 16
Z = ZH * ZL
REL = ("zh", "zl", "core")
REP = ("y", "x")
LINE = ("zh", "zl")
STEPS = (0, 1, 2, 3)
EXTRA = 16
F32 = jnp.float32
BF16 = jnp.bfloat16


def exchange(blocks, axis):
    return lax.all_to_all(blocks, axis, split_axis=0, concat_axis=0, tiled=True)


def spread(block, axis, count):
    return exchange(jnp.broadcast_to(block[None], (count,) + block.shape), axis)


def near_by(step, core):
    return jnp.where(step == 2, 2 - 4 * core, jnp.where(step == 3, -1, step))


def near_move(block, step):
    pairs = []
    for z in range(Z):
        for core in range(CORES):
            by = (0, 1, 2 - 4 * core, -1)[step]
            pairs.append((z * CORES + core, (z + by) % Z * CORES + core))
    return lax.ppermute(block, REL, pairs)


def far_move(block, step):
    return lax.ppermute(block, LINE, [(z, (z + 4 * step) % Z) for z in range(Z)])


def swap_core(block):
    return lax.ppermute(block, "core", [(0, 1), (1, 0)])


def dot(a, b, over):
    return lax.dot_general(a, b, (over, ((), ())), preferred_element_type=F32)


NN, NT, TN = ((1,), (0,)), ((1,), (1,)), ((0,), (0,))


def order_kernel(
    per_owner, mine, cap, fill, owners, rel_emb, core, head_ids, tail_ids, rel_ids, ents,
    part, ordered, order_sel, slot_of, sent, own, wide
):
    step = pl.program_id(0)
    rels = owners.shape[1]
    block = core.shape[0]
    rows_dev = wide.shape[0] // mine

    @pl.when(step == 0)
    def _():
        fill_send(cap, fill, head_ids, tail_ids, rel_ids, ents, sent)
        owner = owners[...].astype(F32)
        count = rels // per_owner
        has = lax.broadcasted_iota(jnp.int32, (count, rels), 0).astype(F32) == owner
        has = jnp.where(has, 1.0, 0.0).astype(BF16)
        same = dot(has, has, TN)
        index = lax.broadcasted_iota(jnp.int32, (rels, rels), 0)
        before = index < lax.broadcasted_iota(jnp.int32, (rels, rels), 1)
        rank = jnp.sum(jnp.where(before, same, 0.0), axis=0, keepdims=True)
        slot = owner * per_owner + rank
        slot_of[...] = slot
        chosen = jnp.where(index.astype(F32) == slot, 1.0, 0.0).astype(BF16)
        quarter = lax.broadcasted_iota(jnp.int32, (rels // 4, rels), 0)
        for i in range(4):
            order_sel[i] = jnp.where((quarter * 4 + i).astype(F32) == slot, 1.0, 0.0).astype(BF16)
        ordered[...] = dot(chosen, rel_emb[...], NN).astype(BF16)
        first = (lax.axis_index(REP) * mine + lax.broadcasted_iota(jnp.int32, own.shape[:1] + (rels,), 0)).astype(F32)
        own[...] = dot(jnp.where(first == slot, 1.0, 0.0).astype(BF16), rel_emb[...], NN).astype(BF16)

    for a in range(block):
        rows = dot(own[...], core[a], NN)
        for w in range(mine):
            wide[pl.ds(w * rows_dev + step * block + a, 1), :] = rows[w : w + 1]

    @pl.when(step == pl.num_programs(0) - 1)
    def _():
        part[...] = wide[...].astype(BF16)


def fill_send(cap, fill, head_ids, tail_ids, rel_ids, ents, out):
    ent_rows = ents.shape[0]
    lane = lax.broadcasted_iota(jnp.int32, (1, 128), 1)
    limits = []
    for row in range(8):
        limit = jnp.full((1, 128), fill[0, row * 128 // cap], jnp.int32)
        for at in range(cap, 128, cap):
            limit = jnp.where(lane >= at, fill[0, (row * 128 + at) // cap], limit)
        limits.append(limit)
    numbers = [head_ids[...], tail_ids[...], rel_ids[...], jnp.concatenate(limits, axis=0)]
    numbers = jnp.concatenate([a.astype(F32) for a in numbers], axis=1)
    numbers = jnp.concatenate([numbers, jnp.zeros_like(numbers)], axis=0).astype(BF16)
    for s in range(out.shape[0]):
        out[s, :ent_rows, :] = ents[...]
        out[s, ent_rows:, :] = numbers


def hot_of(ids, ent_rows):
    entity = lax.broadcasted_iota(jnp.int32, (ent_rows, ids.shape[1]), 0).astype(F32)
    return jnp.where(entity == ids, 1.0, 0.0).astype(BF16)


def gather_kernel(cap, where, slot_of, table, ids, heads, tails):
    ent_rows = table.shape[1] - EXTRA
    own = tails.shape[0]
    kinds = heads.shape[0] // own
    seats = own * cap
    columns = (kinds + 1) * seats
    g = where[0]
    row = lax.broadcasted_iota(jnp.int32, (EXTRA, 512), 0)
    lines = []
    for s in range(table.shape[0]):
        line = table[s, ent_rows:, :].astype(F32)
        lines.append(jnp.sum(jnp.where(row == g * seats // 128, line, 0.0), axis=0, keepdims=True))
    lines = jnp.concatenate(lines, axis=0)
    lines = [lines[:, i * 128 : (i + 1) * 128] for i in range(4)]
    head, tail, relation, limit = [
        jnp.where(g * seats % 128 == 0, line[:, :seats], line[:, 128 - seats :]) for line in lines
    ]
    seat = lax.broadcasted_iota(jnp.int32, head.shape, 1)
    live = (seat % cap).astype(F32) < limit
    slot = slot_of[...]
    relations = lax.broadcasted_iota(jnp.int32, slot.shape, 1).astype(F32)
    found = []
    for w in range(kinds):
        name = None
        for o in range(own):
            mine = (g * own * kinds + o * kinds + w).astype(F32)
            this = jnp.sum(jnp.where(slot == mine, relations, 0.0), axis=1, keepdims=True)
            this = jnp.broadcast_to(this, head.shape)
            name = this if name is None else jnp.where(seat >= o * cap, this, name)
        found.append(jnp.where(live & (relation == name), head, -1.0))
    found.append(jnp.where(live, tail, -1.0))
    ids[...] = jnp.concatenate(found + [jnp.full(head.shape, -1.0, F32)], axis=1)
    for s in range(table.shape[0]):
        hot = hot_of(ids[s : s + 1, :columns], ent_rows)
        rows = dot(hot, table[s, :ent_rows, :], TN).astype(BF16)
        for kind in range(kinds + 1):
            for o in range(own):
                at = (kind * own + o) * cap
                block = rows[at : at + cap]
                if kind < kinds:
                    heads[o * kinds + kind, s * cap : (s + 1) * cap, :] = block
                else:
                    tails[o, s * cap : (s + 1) * cap, :] = block


def score_kernel(scale, rows_dev, starts, heads, tails, half, other, pool, mats, dquery, dtail, given, kept, dm, dp):
    own = tails.shape[0]
    kinds = heads.shape[0] // own
    mine = heads.shape[0]
    for i in range(half.shape[0]):
        for which, source in ((0, half), (1, other)):
            at = pl.multiple_of(starts[which, i], rows_dev)
            for w in range(mine):
                mats[w, pl.ds(at, rows_dev), :] = source[i, w * rows_dev : (w + 1) * rows_dev, :]
    negatives = pool[...]
    total = None
    for o in range(own):
        query = dot(heads[o * kinds], mats[o * kinds], NN)
        for w in range(1, kinds):
            query = query + dot(heads[o * kinds + w], mats[o * kinds + w], NN)
        query = query.astype(BF16)
        qfloat = query.astype(F32)
        tail = tails[o].astype(F32)
        gpos = -jax.nn.sigmoid(-jnp.sum(qfloat * tail, axis=1, keepdims=True)) * scale
        gneg = (jax.nn.sigmoid(dot(query, negatives, NT)) * (scale / pool.shape[0])).astype(BF16)
        grad = (gpos * tail + dot(gneg, negatives, NN)).astype(BF16)
        dquery[o] = grad
        dtail[o] = (gpos * qfloat).astype(BF16)
        piece = dot(gneg, query, TN)
        total = piece if total is None else total + piece
        for w in range(kinds):
            dm[o * kinds + w] = dot(heads[o * kinds + w], grad, TN).astype(BF16)
    dp[...] = total
    pool_dev = rows_dev // 2
    for which, target in ((2, kept), (3, given)):
        for s in range(4):
            pieces = []
            for p in range(4):
                at = pl.multiple_of(starts[which, s * 4 + p], rows_dev)
                for w in range(mine):
                    row = (p * mine + w) * rows_dev
                    target[s, row : row + rows_dev, :] = dm[w, pl.ds(at, rows_dev), :]
                at = pl.multiple_of(starts[which, s * 4 + p] // 2, pool_dev)
                pieces.append(dp[pl.ds(at, pool_dev), :])
            target[s, 4 * mine * rows_dev :, :] = jnp.concatenate(pieces, axis=0).astype(BF16)


def scatter_kernel(cap, ids, dquery, dtail, mats, out, dheads):
    own = dquery.shape[0]
    kinds = mats.shape[0] // own
    columns = (kinds + 1) * own * cap
    ent_rows = out.shape[1]
    for o in range(own):
        for w in range(kinds):
            dheads[o * kinds + w] = dot(dquery[o], mats[o * kinds + w], NT).astype(BF16)
    for s in range(out.shape[0]):
        hot = hot_of(ids[s : s + 1, :columns], ent_rows)
        at = slice(s * cap, (s + 1) * cap)
        grads = [dheads[o * kinds + w, at, :] for w in range(kinds) for o in range(own)]
        grads += [dtail[o, at, :] for o in range(own)]
        out[s] = dot(hot, jnp.concatenate(grads, axis=0), NN).astype(BF16)


def core_kernel(rows_dev, ordered, sums, out, wide):
    rels = ordered.shape[0]
    each = rels // sums.shape[0] * rows_dev
    lanes = wide.shape[0]
    for s in range(sums.shape[0]):
        rows = sums[s, :each, :].astype(F32)
        for lane in range(lanes):
            wide[lane, s * each : (s + 1) * each, :] = rows[:, lane * 128 : (lane + 1) * 128]
    weights = ordered[...]
    for a in range(rows_dev):
        rows = [wide[lane, pl.ds(a, rels, stride=rows_dev), :] for lane in range(lanes)]
        out[a] = dot(weights, jnp.concatenate(rows, axis=1).astype(BF16), TN).astype(BF16)


def last_kernel(where, own, other, order_sel, rel_grad, pool_grad):
    rel_rows = order_sel.shape[1]
    pool_dev = own.shape[1] - rel_rows
    first = where[1] == 0
    total = None
    for s in range(own.shape[0]):
        mine, theirs = own[s].astype(F32), other[s].astype(F32)
        both = mine[:rel_rows] + theirs[:rel_rows]
        total = both if total is None else total + both
        mine, theirs = mine[rel_rows:], theirs[rel_rows:]
        rows = [jnp.where(first, mine, theirs), jnp.where(first, theirs, mine)]
        at = 2 * pool_dev * s
        pool_grad[at : at + 2 * pool_dev, :] = jnp.concatenate(rows, axis=0).astype(BF16)
    total = total.astype(BF16)
    grad = None
    for i in range(4):
        piece = dot(order_sel[i], total[:, i * 128 : (i + 1) * 128], TN)
        grad = piece if grad is None else grad + piece
    rel_grad[...] = grad


def call(kernel, outs, flops, in_specs, scratch=(), dtypes=None):
    vmem = pl.BlockSpec(memory_space=pltpu.VMEM)
    return pl.pallas_call(
        kernel,
        out_shape=tuple(
            jax.ShapeDtypeStruct(shape, dtype) for shape, dtype in zip(outs, dtypes or [BF16] * len(outs))
        ),
        in_specs=in_specs,
        out_specs=tuple(vmem for _ in outs),
        scratch_shapes=scratch,
        cost_estimate=pl.CostEstimate(flops=flops, bytes_accessed=1 << 23, transcendentals=0),
        compiler_params=pltpu.CompilerParams(vmem_limit_bytes=40 << 20),
    )


def body(core, rel_emb, ents, pool, owner_of, rel_ids, head_ids, tail_ids, fill):
    rels, feats_rel = rel_emb.shape
    rows_dev, _, feats = core.shape
    owners = fill.shape[1]
    cap = rel_ids.shape[0] // owners
    per_owner = rels // owners
    own = owners // REPS
    mine = own * per_owner
    seats = own * cap
    ent_rows = ents.shape[0]
    pool_rows = pool.shape[0]
    pool_dev = pool_rows // (Z * CORES)
    scale = 1.0 / REPS
    g = lax.axis_index(REP)
    z = lax.axis_index(LINE)
    c = lax.axis_index("core")

    vmem = pl.BlockSpec(memory_space=pltpu.VMEM)
    smem = pl.BlockSpec(memory_space=pltpu.SMEM)
    slots = REPS * cap
    block = slots * feats * feats * 2
    where = jnp.stack([g, c]).astype(jnp.int32)
    shapes = (
        (mine * rows_dev, feats),
        (rels, feats_rel),
        (4, rels // 4, rels),
        (1, rels),
        (REPS, ent_rows + EXTRA, feats),
    )
    lines = (slots * own // 128, 128)
    steps = 1
    part, ordered, order_sel, slot_of, sent = pl.pallas_call(
        functools.partial(order_kernel, per_owner, mine, cap),
        grid=(steps,),
        out_shape=tuple(
            jax.ShapeDtypeStruct(shape, dtype) for shape, dtype in zip(shapes, (BF16, BF16, BF16, F32, BF16))
        ),
        in_specs=[
            smem,
            pl.BlockSpec((1, rels), lambda i: (0, 0)),
            pl.BlockSpec((rels, feats_rel), lambda i: (0, 0)),
            pl.BlockSpec((rows_dev // steps, feats_rel, feats), lambda i: (i, 0, 0)),
            pl.BlockSpec(lines, lambda i: (0, 0)),
            pl.BlockSpec(lines, lambda i: (0, 0)),
            pl.BlockSpec(lines, lambda i: (0, 0)),
            pl.BlockSpec((ent_rows, feats), lambda i: (0, 0)),
        ],
        out_specs=tuple(pl.BlockSpec(shape, lambda i, n=len(shape): (0,) * n) for shape in shapes),
        scratch_shapes=(pltpu.VMEM((16, feats_rel), BF16), pltpu.VMEM((mine * rows_dev, feats), F32)),
        cost_estimate=pl.CostEstimate(flops=16 * 2 * core.size, bytes_accessed=1 << 21, transcendentals=0),
        compiler_params=pltpu.CompilerParams(vmem_limit_bytes=60 << 20),
    )(
        fill,
        owner_of.reshape(1, rels),
        rel_emb,
        core,
        *(a.reshape(lines) for a in (head_ids, tail_ids, rel_ids)),
        ents,
    )

    table = exchange(sent, REP)

    far = jnp.stack([part] + [far_move(part, p) for p in STEPS[1:]])
    half = jnp.concatenate([far] + [near_move(far, s) for s in STEPS[1:]])
    other = swap_core(half)

    ids, heads, tails = call(
        functools.partial(gather_kernel, cap),
        ((REPS, 4 * seats), (mine, slots, feats), (own, slots, feats)),
        REPS * 3 * seats * ent_rows * feats * 2,
        [smem, vmem, vmem],
        dtypes=(F32, BF16, BF16),
    )(where, slot_of, table)

    entry = jnp.arange(Z, dtype=jnp.int32)
    starts = []
    for sign in (-1, 1):
        for core_of in (c, 1 - c):
            chip = (z + sign * (near_by(entry // 4, core_of) + 4 * (entry % 4))) % Z
            starts.append((chip * CORES + core_of) * rows_dev)
    starts = jnp.stack(starts)

    split = 4 * mine * rows_dev
    sum_rows = split + 4 * pool_dev
    mats, dquery, dtail, given, kept = call(
        functools.partial(score_kernel, scale, rows_dev),
        (
            (mine, feats, feats),
            (own, slots, feats),
            (own, slots, feats),
            (4, sum_rows, feats),
            (4, sum_rows, feats),
        ),
        2 * mine * block + 3 * own * block // 2,
        [smem] + [vmem] * 5,
        (pltpu.VMEM((mine, feats, feats), BF16), pltpu.VMEM((pool_rows, feats), F32)),
    )(starts, heads, tails, half, other, pool)

    (sent,) = call(
        functools.partial(scatter_kernel, cap),
        ((REPS, ent_rows, feats),),
        mine * block + REPS * 3 * seats * ent_rows * feats * 2,
        [vmem] * 4,
        (pltpu.VMEM((mine, slots, feats), BF16),),
    )(ids, dquery, dtail, mats)

    given, sent = lax.optimization_barrier((swap_core(given), sent))
    back = exchange(sent, REP)
    pair = (kept.astype(F32) + given.astype(F32)).astype(BF16)
    total = pair[0].astype(F32)
    for s in STEPS[1:]:
        total = total + near_move(pair[s], s).astype(F32)
    total = total.astype(BF16)
    each = mine * rows_dev
    blocks = [
        jnp.concatenate(
            [
                total[p * each : (p + 1) * each],
                total[split + p * pool_dev : split + (p + 1) * pool_dev],
            ]
        )
        for p in STEPS
    ]
    own_sum = blocks[0].astype(F32)
    for p in STEPS[1:]:
        own_sum = own_sum + far_move(blocks[p], p).astype(F32)
    own_sum, back = lax.optimization_barrier((own_sum.astype(BF16), back))
    ent_grad = jnp.sum(back.astype(F32), axis=0).astype(BF16)

    sums = spread(own_sum, REP, REPS)
    rel_own = jnp.einsum(
        "gwab,akb->gwk",
        sums[:, :each].reshape(REPS, mine, rows_dev, feats),
        core,
        preferred_element_type=F32,
    ).astype(BF16)
    pool_own = jnp.sum(sums[:, each:].astype(F32), axis=0).astype(BF16)

    rel_rows = rels * feats_rel // feats
    small = spread(jnp.concatenate([rel_own.reshape(rel_rows, feats), pool_own]), LINE, Z)
    (core_grad,) = call(
        functools.partial(core_kernel, rows_dev),
        ((rows_dev, feats_rel, feats),),
        2 * rows_dev * feats_rel * rels * feats,
        [vmem] * 2,
        (pltpu.VMEM((feats // 128, rels * rows_dev, 128), F32),),
    )(ordered, sums)
    small, core_grad, ent_grad = lax.optimization_barrier((small, core_grad, ent_grad))
    rel_grad, pool_grad = call(
        last_kernel,
        ((rels, feats_rel), (pool_rows, feats)),
        1 << 20,
        [smem] + [vmem] * 3,
        dtypes=(F32, BF16),
    )(where, small, swap_core(small), order_sel)
    return (core_grad, rel_grad, ent_grad, pool_grad)


def solution(mesh):
    cut = Mesh(mesh.devices.reshape(ZH, ZL, CORES, 4, 4), REL + REP)
    whole = REL + REP
    return jax.shard_map(
        body,
        mesh=cut,
        in_specs=(
            P(REL, None, None),
            P(),
            P(whole, None),
            P(),
            P(),
            P(whole),
            P(whole),
            P(whole),
            P(whole, None),
        ),
        out_specs=(P(REL, None, None), P(), P(whole, None), P()),
        check_vma=False,
    )
```

```python
import functools

import jax
import jax.numpy as jnp
from jax import lax
from jax.experimental import pallas as pl
from jax.experimental.pallas import tpu as pltpu
from jax.sharding import Mesh, PartitionSpec as P

ZH, ZL, CORES, REPS = 4, 4, 2, 16
Z = ZH * ZL
REL = ("zh", "zl", "core")
REP = ("y", "x")
LINE = ("zh", "zl")
STEPS = (0, 1, 2, 3)
EXTRA = 8
F32 = jnp.float32
BF16 = jnp.bfloat16


def exchange(blocks, axis):
    return lax.all_to_all(blocks, axis, split_axis=0, concat_axis=0, tiled=True)


def spread(block, axis, count):
    return exchange(jnp.broadcast_to(block[None], (count,) + block.shape), axis)


def near_by(step, core):
    return jnp.where(step == 2, 2 - 4 * core, jnp.where(step == 3, -1, step))


def near_move(block, step):
    pairs = []
    for z in range(Z):
        for core in range(CORES):
            by = (0, 1, 2 - 4 * core, -1)[step]
            pairs.append((z * CORES + core, (z + by) % Z * CORES + core))
    return lax.ppermute(block, REL, pairs)


def far_move(block, step):
    return lax.ppermute(block, LINE, [(z, (z + 4 * step) % Z) for z in range(Z)])


def swap_core(block):
    return lax.ppermute(block, "core", [(0, 1), (1, 0)])


def dot(a, b, over):
    return lax.dot_general(a, b, (over, ((), ())), preferred_element_type=F32)


NN, NT, TN = ((1,), (0,)), ((1,), (1,)), ((0,), (0,))


def order_kernel(
    per_owner, mine, cap, fill, owners, rel_emb, core, head_ids, tail_ids, rel_ids, ents,
    part, ordered, order_sel, slot_of, sent, own, wide
):
    step = pl.program_id(0)
    rels = owners.shape[1]
    block = core.shape[0]
    rows_dev = wide.shape[0] // mine

    @pl.when(step == 0)
    def _():
        fill_send(cap, fill, head_ids, tail_ids, rel_ids, ents, sent)
        owner = owners[...].astype(F32)
        count = rels // per_owner
        has = lax.broadcasted_iota(jnp.int32, (count, rels), 0).astype(F32) == owner
        has = jnp.where(has, 1.0, 0.0).astype(BF16)
        same = dot(has, has, TN)
        index = lax.broadcasted_iota(jnp.int32, (rels, rels), 0)
        before = index < lax.broadcasted_iota(jnp.int32, (rels, rels), 1)
        rank = jnp.sum(jnp.where(before, same, 0.0), axis=0, keepdims=True)
        slot = owner * per_owner + rank
        slot_of[...] = slot
        chosen = jnp.where(index.astype(F32) == slot, 1.0, 0.0).astype(BF16)
        quarter = lax.broadcasted_iota(jnp.int32, (rels // 4, rels), 0)
        for i in range(4):
            order_sel[i] = jnp.where((quarter * 4 + i).astype(F32) == slot, 1.0, 0.0).astype(BF16)
        ordered[...] = dot(chosen, rel_emb[...], NN).astype(BF16)
        first = (lax.axis_index(REP) * mine + lax.broadcasted_iota(jnp.int32, own.shape[:1] + (rels,), 0)).astype(F32)
        own[...] = dot(jnp.where(first == slot, 1.0, 0.0).astype(BF16), rel_emb[...], NN).astype(BF16)

    for a in range(block):
        rows = dot(own[...], core[a], NN)
        for w in range(mine):
            wide[pl.ds(w * rows_dev + step * block + a, 1), :] = rows[w : w + 1]

    @pl.when(step == pl.num_programs(0) - 1)
    def _():
        part[...] = wide[...].astype(BF16)


def fill_send(cap, fill, head_ids, tail_ids, rel_ids, ents, out):
    ent_rows = ents.shape[0]
    lane = lax.broadcasted_iota(jnp.int32, (1, 128), 1)
    limits = []
    for row in range(8):
        limit = jnp.full((1, 128), fill[0, row * 128 // cap], jnp.int32)
        for at in range(cap, 128, cap):
            limit = jnp.where(lane >= at, fill[0, (row * 128 + at) // cap], limit)
        limits.append(limit)
    numbers = [head_ids[...], tail_ids[...], rel_ids[...], jnp.concatenate(limits, axis=0)]
    numbers = jnp.concatenate([a.astype(F32) for a in numbers], axis=1).astype(BF16)
    for s in range(out.shape[0]):
        out[s, :ent_rows, :] = ents[...]
        out[s, ent_rows:, :] = numbers


def hot_of(ids, ent_rows):
    entity = lax.broadcasted_iota(jnp.int32, (ent_rows, ids.shape[1]), 0).astype(F32)
    return jnp.where(entity == ids, 1.0, 0.0).astype(BF16)


def gather_kernel(cap, where, slot_of, table, ids, heads, tails):
    ent_rows = table.shape[1] - EXTRA
    own = tails.shape[0]
    kinds = heads.shape[0] // own
    seats = own * cap
    columns = (kinds + 1) * seats
    g = where[0]
    row = lax.broadcasted_iota(jnp.int32, (EXTRA, 512), 0)
    lines = []
    for s in range(table.shape[0]):
        line = table[s, ent_rows:, :].astype(F32)
        lines.append(jnp.sum(jnp.where(row == g * seats // 128, line, 0.0), axis=0, keepdims=True))
    lines = jnp.concatenate(lines, axis=0)
    lines = [lines[:, i * 128 : (i + 1) * 128] for i in range(4)]
    head, tail, relation, limit = [
        jnp.where(g * seats % 128 == 0, line[:, :seats], line[:, 128 - seats :]) for line in lines
    ]
    seat = lax.broadcasted_iota(jnp.int32, head.shape, 1)
    live = (seat % cap).astype(F32) < limit
    slot = slot_of[...]
    relations = lax.broadcasted_iota(jnp.int32, slot.shape, 1).astype(F32)
    found = []
    for w in range(kinds):
        name = None
        for o in range(own):
            mine = (g * own * kinds + o * kinds + w).astype(F32)
            this = jnp.sum(jnp.where(slot == mine, relations, 0.0), axis=1, keepdims=True)
            this = jnp.broadcast_to(this, head.shape)
            name = this if name is None else jnp.where(seat >= o * cap, this, name)
        found.append(jnp.where(live & (relation == name), head, -1.0))
    found.append(jnp.where(live, tail, -1.0))
    ids[...] = jnp.concatenate(found + [jnp.full(head.shape, -1.0, F32)], axis=1)
    for s in range(table.shape[0]):
        hot = hot_of(ids[s : s + 1, :columns], ent_rows)
        rows = dot(hot, table[s, :ent_rows, :], TN).astype(BF16)
        for kind in range(kinds + 1):
            for o in range(own):
                at = (kind * own + o) * cap
                block = rows[at : at + cap]
                if kind < kinds:
                    heads[o * kinds + kind, s * cap : (s + 1) * cap, :] = block
                else:
                    tails[o, s * cap : (s + 1) * cap, :] = block


def score_kernel(scale, rows_dev, starts, heads, tails, half, other, pool, mats, dquery, dtail, given, kept, dm, dp):
    own = tails.shape[0]
    kinds = heads.shape[0] // own
    mine = heads.shape[0]
    for i in range(half.shape[0]):
        for which, source in ((0, half), (1, other)):
            at = pl.multiple_of(starts[which, i], rows_dev)
            for w in range(mine):
                mats[w, pl.ds(at, rows_dev), :] = source[i, w * rows_dev : (w + 1) * rows_dev, :]
    negatives = pool[...]
    total = None
    for o in range(own):
        query = dot(heads[o * kinds], mats[o * kinds], NN)
        for w in range(1, kinds):
            query = query + dot(heads[o * kinds + w], mats[o * kinds + w], NN)
        query = query.astype(BF16)
        qfloat = query.astype(F32)
        tail = tails[o].astype(F32)
        gpos = -jax.nn.sigmoid(-jnp.sum(qfloat * tail, axis=1, keepdims=True)) * scale
        gneg = (jax.nn.sigmoid(dot(query, negatives, NT)) * (scale / pool.shape[0])).astype(BF16)
        grad = (gpos * tail + dot(gneg, negatives, NN)).astype(BF16)
        dquery[o] = grad
        dtail[o] = (gpos * qfloat).astype(BF16)
        piece = dot(gneg, query, TN)
        total = piece if total is None else total + piece
        for w in range(kinds):
            dm[o * kinds + w] = dot(heads[o * kinds + w], grad, TN).astype(BF16)
    dp[...] = total
    pool_dev = rows_dev // 2
    for which, target in ((2, kept), (3, given)):
        for s in range(4):
            pieces = []
            for p in range(4):
                at = pl.multiple_of(starts[which, s * 4 + p], rows_dev)
                for w in range(mine):
                    row = (p * mine + w) * rows_dev
                    target[s, row : row + rows_dev, :] = dm[w, pl.ds(at, rows_dev), :]
                at = pl.multiple_of(starts[which, s * 4 + p] // 2, pool_dev)
                pieces.append(dp[pl.ds(at, pool_dev), :])
            target[s, 4 * mine * rows_dev :, :] = jnp.concatenate(pieces, axis=0).astype(BF16)


def scatter_kernel(cap, ids, dquery, dtail, mats, out, dheads):
    own = dquery.shape[0]
    kinds = mats.shape[0] // own
    columns = (kinds + 1) * own * cap
    ent_rows = out.shape[1]
    for o in range(own):
        for w in range(kinds):
            dheads[o * kinds + w] = dot(dquery[o], mats[o * kinds + w], NT).astype(BF16)
    for s in range(out.shape[0]):
        hot = hot_of(ids[s : s + 1, :columns], ent_rows)
        at = slice(s * cap, (s + 1) * cap)
        grads = [dheads[o * kinds + w, at, :] for w in range(kinds) for o in range(own)]
        grads += [dtail[o, at, :] for o in range(own)]
        out[s] = dot(hot, jnp.concatenate(grads, axis=0), NN).astype(BF16)


def core_kernel(rows_dev, ordered, sums, out, wide):
    rels = ordered.shape[0]
    each = rels // sums.shape[0] * rows_dev
    lanes = wide.shape[0]
    for s in range(sums.shape[0]):
        rows = sums[s, :each, :].astype(F32)
        for lane in range(lanes):
            wide[lane, s * each : (s + 1) * each, :] = rows[:, lane * 128 : (lane + 1) * 128]
    weights = ordered[...]
    for a in range(rows_dev):
        rows = [wide[lane, pl.ds(a, rels, stride=rows_dev), :] for lane in range(lanes)]
        out[a] = dot(weights, jnp.concatenate(rows, axis=1).astype(BF16), TN).astype(BF16)


def last_kernel(where, own, other, order_sel, rel_grad, pool_grad):
    rel_rows = order_sel.shape[1]
    pool_dev = own.shape[1] - rel_rows
    first = where[1] == 0
    total = None
    for s in range(own.shape[0]):
        mine, theirs = own[s].astype(F32), other[s].astype(F32)
        both = mine[:rel_rows] + theirs[:rel_rows]
        total = both if total is None else total + both
        mine, theirs = mine[rel_rows:], theirs[rel_rows:]
        rows = [jnp.where(first, mine, theirs), jnp.where(first, theirs, mine)]
        at = 2 * pool_dev * s
        pool_grad[at : at + 2 * pool_dev, :] = jnp.concatenate(rows, axis=0).astype(BF16)
    total = total.astype(BF16)
    grad = None
    for i in range(4):
        piece = dot(order_sel[i], total[:, i * 128 : (i + 1) * 128], TN)
        grad = piece if grad is None else grad + piece
    rel_grad[...] = grad


def call(kernel, outs, flops, in_specs, scratch=(), dtypes=None):
    vmem = pl.BlockSpec(memory_space=pltpu.VMEM)
    return pl.pallas_call(
        kernel,
        out_shape=tuple(
            jax.ShapeDtypeStruct(shape, dtype) for shape, dtype in zip(outs, dtypes or [BF16] * len(outs))
        ),
        in_specs=in_specs,
        out_specs=tuple(vmem for _ in outs),
        scratch_shapes=scratch,
        cost_estimate=pl.CostEstimate(flops=flops, bytes_accessed=1 << 23, transcendentals=0),
        compiler_params=pltpu.CompilerParams(vmem_limit_bytes=40 << 20),
    )


def body(core, rel_emb, ents, pool, owner_of, rel_ids, head_ids, tail_ids, fill):
    rels, feats_rel = rel_emb.shape
    rows_dev, _, feats = core.shape
    owners = fill.shape[1]
    cap = rel_ids.shape[0] // owners
    per_owner = rels // owners
    own = owners // REPS
    mine = own * per_owner
    seats = own * cap
    ent_rows = ents.shape[0]
    pool_rows = pool.shape[0]
    pool_dev = pool_rows // (Z * CORES)
    scale = 1.0 / REPS
    g = lax.axis_index(REP)
    z = lax.axis_index(LINE)
    c = lax.axis_index("core")

    vmem = pl.BlockSpec(memory_space=pltpu.VMEM)
    smem = pl.BlockSpec(memory_space=pltpu.SMEM)
    slots = REPS * cap
    block = slots * feats * feats * 2
    where = jnp.stack([g, c]).astype(jnp.int32)
    shapes = (
        (mine * rows_dev, feats),
        (rels, feats_rel),
        (4, rels // 4, rels),
        (1, rels),
        (REPS, ent_rows + EXTRA, feats),
    )
    lines = (slots * own // 128, 128)
    steps = 1
    part, ordered, order_sel, slot_of, sent = pl.pallas_call(
        functools.partial(order_kernel, per_owner, mine, cap),
        grid=(steps,),
        out_shape=tuple(
            jax.ShapeDtypeStruct(shape, dtype) for shape, dtype in zip(shapes, (BF16, BF16, BF16, F32, BF16))
        ),
        in_specs=[
            smem,
            pl.BlockSpec((1, rels), lambda i: (0, 0)),
            pl.BlockSpec((rels, feats_rel), lambda i: (0, 0)),
            pl.BlockSpec((rows_dev // steps, feats_rel, feats), lambda i: (i, 0, 0)),
            pl.BlockSpec(lines, lambda i: (0, 0)),
            pl.BlockSpec(lines, lambda i: (0, 0)),
            pl.BlockSpec(lines, lambda i: (0, 0)),
            pl.BlockSpec((ent_rows, feats), lambda i: (0, 0)),
        ],
        out_specs=tuple(pl.BlockSpec(shape, lambda i, n=len(shape): (0,) * n) for shape in shapes),
        scratch_shapes=(pltpu.VMEM((16, feats_rel), BF16), pltpu.VMEM((mine * rows_dev, feats), F32)),
        cost_estimate=pl.CostEstimate(flops=16 * 2 * core.size, bytes_accessed=1 << 21, transcendentals=0),
        compiler_params=pltpu.CompilerParams(vmem_limit_bytes=60 << 20),
    )(
        fill,
        owner_of.reshape(1, rels),
        rel_emb,
        core,
        *(a.reshape(lines) for a in (head_ids, tail_ids, rel_ids)),
        ents,
    )

    table = exchange(sent, REP)

    far = jnp.stack([part] + [far_move(part, p) for p in STEPS[1:]])
    half = jnp.concatenate([far] + [near_move(far, s) for s in STEPS[1:]])
    other = swap_core(half)

    ids, heads, tails = call(
        functools.partial(gather_kernel, cap),
        ((REPS, 4 * seats), (mine, slots, feats), (own, slots, feats)),
        REPS * 3 * seats * ent_rows * feats * 2,
        [smem, vmem, vmem],
        dtypes=(F32, BF16, BF16),
    )(where, slot_of, table)

    entry = jnp.arange(Z, dtype=jnp.int32)
    starts = []
    for sign in (-1, 1):
        for core_of in (c, 1 - c):
            chip = (z + sign * (near_by(entry // 4, core_of) + 4 * (entry % 4))) % Z
            starts.append((chip * CORES + core_of) * rows_dev)
    starts = jnp.stack(starts)

    split = 4 * mine * rows_dev
    sum_rows = split + 4 * pool_dev
    mats, dquery, dtail, given, kept = call(
        functools.partial(score_kernel, scale, rows_dev),
        (
            (mine, feats, feats),
            (own, slots, feats),
            (own, slots, feats),
            (4, sum_rows, feats),
            (4, sum_rows, feats),
        ),
        2 * mine * block + 3 * own * block // 2,
        [smem] + [vmem] * 5,
        (pltpu.VMEM((mine, feats, feats), BF16), pltpu.VMEM((pool_rows, feats), F32)),
    )(starts, heads, tails, half, other, pool)

    (sent,) = call(
        functools.partial(scatter_kernel, cap),
        ((REPS, ent_rows, feats),),
        mine * block + REPS * 3 * seats * ent_rows * feats * 2,
        [vmem] * 4,
        (pltpu.VMEM((mine, slots, feats), BF16),),
    )(ids, dquery, dtail, mats)

    given, sent = lax.optimization_barrier((swap_core(given), sent))
    back = exchange(sent, REP)
    pair = (kept.astype(F32) + given.astype(F32)).astype(BF16)
    total = pair[0].astype(F32)
    for s in STEPS[1:]:
        total = total + near_move(pair[s], s).astype(F32)
    total = total.astype(BF16)
    each = mine * rows_dev
    blocks = [
        jnp.concatenate(
            [
                total[p * each : (p + 1) * each],
                total[split + p * pool_dev : split + (p + 1) * pool_dev],
            ]
        )
        for p in STEPS
    ]
    own_sum = blocks[0].astype(F32)
    for p in STEPS[1:]:
        own_sum = own_sum + far_move(blocks[p], p).astype(F32)
    own_sum, back = lax.optimization_barrier((own_sum.astype(BF16), back))
    ent_grad = jnp.sum(back.astype(F32), axis=0).astype(BF16)

    sums = spread(own_sum, REP, REPS)
    rel_own = jnp.einsum(
        "gwab,akb->gwk",
        sums[:, :each].reshape(REPS, mine, rows_dev, feats),
        core,
        preferred_element_type=F32,
    ).astype(BF16)
    pool_own = jnp.sum(sums[:, each:].astype(F32), axis=0).astype(BF16)

    rel_rows = rels * feats_rel // feats
    small = spread(jnp.concatenate([rel_own.reshape(rel_rows, feats), pool_own]), LINE, Z)
    (core_grad,) = call(
        functools.partial(core_kernel, rows_dev),
        ((rows_dev, feats_rel, feats),),
        2 * rows_dev * feats_rel * rels * feats,
        [vmem] * 2,
        (pltpu.VMEM((feats // 128, rels * rows_dev, 128), F32),),
    )(ordered, sums)
    small, core_grad, ent_grad = lax.optimization_barrier((small, core_grad, ent_grad))
    rel_grad, pool_grad = call(
        last_kernel,
        ((rels, feats_rel), (pool_rows, feats)),
        1 << 20,
        [smem] + [vmem] * 3,
        dtypes=(F32, BF16),
    )(where, small, swap_core(small), order_sel)
    return (core_grad, rel_grad, ent_grad, pool_grad)


def solution(mesh):
    cut = Mesh(mesh.devices.reshape(ZH, ZL, CORES, 4, 4), REL + REP)
    whole = REL + REP
    return jax.shard_map(
        body,
        mesh=cut,
        in_specs=(
            P(REL, None, None),
            P(),
            P(whole, None),
            P(),
            P(),
            P(whole),
            P(whole),
            P(whole),
            P(whole, None),
        ),
        out_specs=(P(REL, None, None), P(), P(whole, None), P()),
        check_vma=False,
    )
```

```python
import functools

import jax
import jax.numpy as jnp
from jax import lax
from jax.experimental import pallas as pl
from jax.experimental.pallas import tpu as pltpu
from jax.sharding import Mesh, PartitionSpec as P

ZH, ZL, CORES, REPS = 4, 4, 2, 16
Z = ZH * ZL
REL = ("zh", "zl", "core")
REP = ("y", "x")
LINE = ("zh", "zl")
STEPS = (0, 1, 2, 3)
EXTRA = 16
F32 = jnp.float32
BF16 = jnp.bfloat16


def exchange(blocks, axis):
    return lax.all_to_all(blocks, axis, split_axis=0, concat_axis=0, tiled=True)


def spread(block, axis, count):
    return exchange(jnp.broadcast_to(block[None], (count,) + block.shape), axis)


def near_by(step, core):
    return jnp.where(step == 2, 2 - 4 * core, jnp.where(step == 3, -1, step))


def near_move(block, step):
    pairs = []
    for z in range(Z):
        for core in range(CORES):
            by = (0, 1, 2 - 4 * core, -1)[step]
            pairs.append((z * CORES + core, (z + by) % Z * CORES + core))
    return lax.ppermute(block, REL, pairs)


def far_move(block, step):
    return lax.ppermute(block, LINE, [(z, (z + 4 * step) % Z) for z in range(Z)])


def swap_core(block):
    return lax.ppermute(block, "core", [(0, 1), (1, 0)])


def dot(a, b, over):
    return lax.dot_general(a, b, (over, ((), ())), preferred_element_type=F32)


NN, NT, TN = ((1,), (0,)), ((1,), (1,)), ((0,), (0,))


def order_kernel(
    per_owner, mine, cap, fill, owners, rel_emb, core, head_ids, tail_ids, rel_ids, ents,
    part, ordered, order_sel, slot_of, sent, own, wide
):
    step = pl.program_id(0)
    rels = owners.shape[1]
    block = core.shape[0]
    rows_dev = wide.shape[0] // mine

    @pl.when(step == 0)
    def _():
        fill_send(cap, fill, head_ids, tail_ids, rel_ids, ents, sent)
        owner = owners[...].astype(F32)
        count = rels // per_owner
        has = lax.broadcasted_iota(jnp.int32, (count, rels), 0).astype(F32) == owner
        has = jnp.where(has, 1.0, 0.0).astype(BF16)
        same = dot(has, has, TN)
        index = lax.broadcasted_iota(jnp.int32, (rels, rels), 0)
        before = index < lax.broadcasted_iota(jnp.int32, (rels, rels), 1)
        rank = jnp.sum(jnp.where(before, same, 0.0), axis=0, keepdims=True)
        slot = owner * per_owner + rank
        slot_of[...] = slot
        chosen = jnp.where(index.astype(F32) == slot, 1.0, 0.0).astype(BF16)
        quarter = lax.broadcasted_iota(jnp.int32, (rels // 4, rels), 0)
        for i in range(4):
            order_sel[i] = jnp.where((quarter * 4 + i).astype(F32) == slot, 1.0, 0.0).astype(BF16)
        ordered[...] = dot(chosen, rel_emb[...], NN).astype(BF16)
        first = (lax.axis_index(REP) * mine + lax.broadcasted_iota(jnp.int32, own.shape[:1] + (rels,), 0)).astype(F32)
        own[...] = dot(jnp.where(first == slot, 1.0, 0.0).astype(BF16), rel_emb[...], NN).astype(BF16)

    for a in range(block):
        rows = dot(own[...], core[a], NN)
        for w in range(mine):
            wide[pl.ds(w * rows_dev + step * block + a, 1), :] = rows[w : w + 1]

    @pl.when(step == pl.num_programs(0) - 1)
    def _():
        part[...] = wide[...].astype(BF16)


def fill_send(cap, fill, head_ids, tail_ids, rel_ids, ents, out):
    ent_rows = ents.shape[0]
    lane = lax.broadcasted_iota(jnp.int32, (1, 128), 1)
    limits = []
    for row in range(8):
        limit = jnp.full((1, 128), fill[0, row * 128 // cap], jnp.int32)
        for at in range(cap, 128, cap):
            limit = jnp.where(lane >= at, fill[0, (row * 128 + at) // cap], limit)
        limits.append(limit)
    numbers = [head_ids[...], tail_ids[...], rel_ids[...], jnp.concatenate(limits, axis=0)]
    numbers = jnp.concatenate([a.astype(F32) for a in numbers], axis=1)
    numbers = jnp.concatenate([numbers, jnp.zeros_like(numbers)], axis=0).astype(BF16)
    for s in range(out.shape[0]):
        out[s, :ent_rows, :] = ents[...]
        out[s, ent_rows:, :] = numbers


def hot_of(ids, ent_rows):
    entity = lax.broadcasted_iota(jnp.int32, (ent_rows, ids.shape[1]), 0).astype(F32)
    return jnp.where(entity == ids, 1.0, 0.0).astype(BF16)


def gather_kernel(cap, where, slot_of, table, ids, heads, tails):
    ent_rows = table.shape[1] - EXTRA
    own = tails.shape[0]
    kinds = heads.shape[0] // own
    seats = own * cap
    columns = (kinds + 1) * seats
    g = where[0]
    row = lax.broadcasted_iota(jnp.int32, (EXTRA, 512), 0)
    lines = []
    for s in range(table.shape[0]):
        line = table[s, ent_rows:, :].astype(F32)
        lines.append(jnp.sum(jnp.where(row == g * seats // 128, line, 0.0), axis=0, keepdims=True))
    lines = jnp.concatenate(lines, axis=0)
    lines = [lines[:, i * 128 : (i + 1) * 128] for i in range(4)]
    head, tail, relation, limit = [
        jnp.where(g * seats % 128 == 0, line[:, :seats], line[:, 128 - seats :]) for line in lines
    ]
    seat = lax.broadcasted_iota(jnp.int32, head.shape, 1)
    live = (seat % cap).astype(F32) < limit
    slot = slot_of[...]
    relations = lax.broadcasted_iota(jnp.int32, slot.shape, 1).astype(F32)
    found = []
    for w in range(kinds):
        name = None
        for o in range(own):
            mine = (g * own * kinds + o * kinds + w).astype(F32)
            this = jnp.sum(jnp.where(slot == mine, relations, 0.0), axis=1, keepdims=True)
            this = jnp.broadcast_to(this, head.shape)
            name = this if name is None else jnp.where(seat >= o * cap, this, name)
        found.append(jnp.where(live & (relation == name), head, -1.0))
    found.append(jnp.where(live, tail, -1.0))
    ids[...] = jnp.concatenate(found + [jnp.full(head.shape, -1.0, F32)], axis=1)
    for s in range(table.shape[0]):
        hot = hot_of(ids[s : s + 1, :columns], ent_rows)
        rows = dot(hot, table[s, :ent_rows, :], TN).astype(BF16)
        for kind in range(kinds + 1):
            for o in range(own):
                at = (kind * own + o) * cap
                block = rows[at : at + cap]
                if kind < kinds:
                    heads[o * kinds + kind, s * cap : (s + 1) * cap, :] = block
                else:
                    tails[o, s * cap : (s + 1) * cap, :] = block


def score_kernel(scale, rows_dev, starts, heads, tails, half, other, pool, mats, dquery, dtail, given, kept, dm, dp):
    own = tails.shape[0]
    kinds = heads.shape[0] // own
    mine = heads.shape[0]
    for i in range(half.shape[0]):
        for which, source in ((0, half), (1, other)):
            at = pl.multiple_of(starts[which, i], rows_dev)
            for w in range(mine):
                mats[w, pl.ds(at, rows_dev), :] = source[i, w * rows_dev : (w + 1) * rows_dev, :]
    negatives = pool[...]
    total = None
    for o in range(own):
        query = dot(heads[o * kinds], mats[o * kinds], NN)
        for w in range(1, kinds):
            query = query + dot(heads[o * kinds + w], mats[o * kinds + w], NN)
        query = query.astype(BF16)
        qfloat = query.astype(F32)
        tail = tails[o].astype(F32)
        gpos = -jax.nn.sigmoid(-jnp.sum(qfloat * tail, axis=1, keepdims=True)) * scale
        gneg = (jax.nn.sigmoid(dot(query, negatives, NT)) * (scale / pool.shape[0])).astype(BF16)
        grad = (gpos * tail + dot(gneg, negatives, NN)).astype(BF16)
        dquery[o] = grad
        dtail[o] = (gpos * qfloat).astype(BF16)
        piece = dot(gneg, query, TN)
        total = piece if total is None else total + piece
        for w in range(kinds):
            dm[o * kinds + w] = dot(heads[o * kinds + w], grad, TN).astype(BF16)
    dp[...] = total
    pool_dev = rows_dev // 2
    for which, target in ((2, kept), (3, given)):
        for s in range(4):
            pieces = []
            for p in range(4):
                at = pl.multiple_of(starts[which, s * 4 + p], rows_dev)
                for w in range(mine):
                    row = (p * mine + w) * rows_dev
                    target[s, row : row + rows_dev, :] = dm[w, pl.ds(at, rows_dev), :]
                at = pl.multiple_of(starts[which, s * 4 + p] // 2, pool_dev)
                pieces.append(dp[pl.ds(at, pool_dev), :])
            target[s, 4 * mine * rows_dev :, :] = jnp.concatenate(pieces, axis=0).astype(BF16)


def scatter_kernel(cap, ids, dquery, dtail, mats, out, dheads):
    own = dquery.shape[0]
    kinds = mats.shape[0] // own
    columns = (kinds + 1) * own * cap
    ent_rows = out.shape[1]
    for o in range(own):
        for w in range(kinds):
            dheads[o * kinds + w] = dot(dquery[o], mats[o * kinds + w], NT).astype(BF16)
    for s in range(out.shape[0]):
        hot = hot_of(ids[s : s + 1, :columns], ent_rows)
        at = slice(s * cap, (s + 1) * cap)
        grads = [dheads[o * kinds + w, at, :] for w in range(kinds) for o in range(own)]
        grads += [dtail[o, at, :] for o in range(own)]
        out[s] = dot(hot, jnp.concatenate(grads, axis=0), NN).astype(BF16)


def core_kernel(rows_dev, ordered, sums, out, wide):
    rels = ordered.shape[0]
    each = rels // sums.shape[0] * rows_dev
    lanes = wide.shape[0]
    for s in range(sums.shape[0]):
        rows = sums[s, :each, :].astype(F32)
        for lane in range(lanes):
            wide[lane, s * each : (s + 1) * each, :] = rows[:, lane * 128 : (lane + 1) * 128]
    weights = ordered[...]
    for a in range(rows_dev):
        rows = [wide[lane, pl.ds(a, rels, stride=rows_dev), :] for lane in range(lanes)]
        out[a] = dot(weights, jnp.concatenate(rows, axis=1).astype(BF16), TN).astype(BF16)


def last_kernel(where, own, other, order_sel, rel_grad, pool_grad):
    rel_rows = order_sel.shape[1]
    pool_dev = own.shape[1] - rel_rows
    first = where[1] == 0
    total = None
    for s in range(own.shape[0]):
        mine, theirs = own[s].astype(F32), other[s].astype(F32)
        both = mine[:rel_rows] + theirs[:rel_rows]
        total = both if total is None else total + both
        mine, theirs = mine[rel_rows:], theirs[rel_rows:]
        rows = [jnp.where(first, mine, theirs), jnp.where(first, theirs, mine)]
        at = 2 * pool_dev * s
        pool_grad[at : at + 2 * pool_dev, :] = jnp.concatenate(rows, axis=0).astype(BF16)
    total = total.astype(BF16)
    grad = None
    for i in range(4):
        piece = dot(order_sel[i], total[:, i * 128 : (i + 1) * 128], TN)
        grad = piece if grad is None else grad + piece
    rel_grad[...] = grad


def call(kernel, outs, flops, in_specs, scratch=(), dtypes=None):
    vmem = pl.BlockSpec(memory_space=pltpu.VMEM)
    return pl.pallas_call(
        kernel,
        out_shape=tuple(
            jax.ShapeDtypeStruct(shape, dtype) for shape, dtype in zip(outs, dtypes or [BF16] * len(outs))
        ),
        in_specs=in_specs,
        out_specs=tuple(vmem for _ in outs),
        scratch_shapes=scratch,
        cost_estimate=pl.CostEstimate(flops=flops, bytes_accessed=1 << 23, transcendentals=0),
        compiler_params=pltpu.CompilerParams(vmem_limit_bytes=40 << 20),
    )


def body(core, rel_emb, ents, pool, owner_of, rel_ids, head_ids, tail_ids, fill):
    rels, feats_rel = rel_emb.shape
    rows_dev, _, feats = core.shape
    owners = fill.shape[1]
    cap = rel_ids.shape[0] // owners
    per_owner = rels // owners
    own = owners // REPS
    mine = own * per_owner
    seats = own * cap
    ent_rows = ents.shape[0]
    pool_rows = pool.shape[0]
    pool_dev = pool_rows // (Z * CORES)
    scale = 1.0 / REPS
    g = lax.axis_index(REP)
    z = lax.axis_index(LINE)
    c = lax.axis_index("core")

    vmem = pl.BlockSpec(memory_space=pltpu.VMEM)
    smem = pl.BlockSpec(memory_space=pltpu.SMEM)
    slots = REPS * cap
    block = slots * feats * feats * 2
    where = jnp.stack([g, c]).astype(jnp.int32)
    shapes = (
        (mine * rows_dev, feats),
        (rels, feats_rel),
        (4, rels // 4, rels),
        (1, rels),
        (REPS, ent_rows + EXTRA, feats),
    )
    lines = (slots * own // 128, 128)
    steps = 1
    part, ordered, order_sel, slot_of, sent = pl.pallas_call(
        functools.partial(order_kernel, per_owner, mine, cap),
        grid=(steps,),
        out_shape=tuple(
            jax.ShapeDtypeStruct(shape, dtype) for shape, dtype in zip(shapes, (BF16, BF16, BF16, F32, BF16))
        ),
        in_specs=[
            smem,
            pl.BlockSpec((1, rels), lambda i: (0, 0)),
            pl.BlockSpec((rels, feats_rel), lambda i: (0, 0)),
            pl.BlockSpec((rows_dev // steps, feats_rel, feats), lambda i: (i, 0, 0)),
            pl.BlockSpec(lines, lambda i: (0, 0)),
            pl.BlockSpec(lines, lambda i: (0, 0)),
            pl.BlockSpec(lines, lambda i: (0, 0)),
            pl.BlockSpec((ent_rows, feats), lambda i: (0, 0)),
        ],
        out_specs=tuple(pl.BlockSpec(shape, lambda i, n=len(shape): (0,) * n) for shape in shapes),
        scratch_shapes=(pltpu.VMEM((16, feats_rel), BF16), pltpu.VMEM((mine * rows_dev, feats), F32)),
        cost_estimate=pl.CostEstimate(flops=16 * 2 * core.size, bytes_accessed=1 << 21, transcendentals=0),
        compiler_params=pltpu.CompilerParams(vmem_limit_bytes=60 << 20),
    )(
        fill,
        owner_of.reshape(1, rels),
        rel_emb,
        core,
        *(a.reshape(lines) for a in (head_ids, tail_ids, rel_ids)),
        ents,
    )

    table = exchange(sent, REP)

    far = jnp.stack([part] + [far_move(part, p) for p in STEPS[1:]])
    half = jnp.concatenate([far] + [near_move(far, s) for s in STEPS[1:]])
    other = swap_core(half)

    ids, heads, tails = call(
        functools.partial(gather_kernel, cap),
        ((REPS, 4 * seats), (mine, slots, feats), (own, slots, feats)),
        REPS * 3 * seats * ent_rows * feats * 2,
        [smem, vmem, vmem],
        dtypes=(F32, BF16, BF16),
    )(where, slot_of, table)

    entry = jnp.arange(Z, dtype=jnp.int32)
    starts = []
    for sign in (-1, 1):
        for core_of in (c, 1 - c):
            chip = (z + sign * (near_by(entry // 4, core_of) + 4 * (entry % 4))) % Z
            starts.append((chip * CORES + core_of) * rows_dev)
    starts = jnp.stack(starts)

    split = 4 * mine * rows_dev
    sum_rows = split + 4 * pool_dev
    mats, dquery, dtail, given, kept = call(
        functools.partial(score_kernel, scale, rows_dev),
        (
            (mine, feats, feats),
            (own, slots, feats),
            (own, slots, feats),
            (4, sum_rows, feats),
            (4, sum_rows, feats),
        ),
        2 * mine * block + 3 * own * block // 2,
        [smem] + [vmem] * 5,
        (pltpu.VMEM((mine, feats, feats), BF16), pltpu.VMEM((pool_rows, feats), F32)),
    )(starts, heads, tails, half, other, pool)

    (sent,) = call(
        functools.partial(scatter_kernel, cap),
        ((REPS, ent_rows, feats),),
        mine * block + REPS * 3 * seats * ent_rows * feats * 2,
        [vmem] * 4,
        (pltpu.VMEM((mine, slots, feats), BF16),),
    )(ids, dquery, dtail, mats)

    given = swap_core(given)
    back = exchange(sent, REP)
    pair = (kept.astype(F32) + given.astype(F32)).astype(BF16)
    total = pair[0].astype(F32)
    for s in STEPS[1:]:
        total = total + near_move(pair[s], s).astype(F32)
    total = total.astype(BF16)
    each = mine * rows_dev
    blocks = [
        jnp.concatenate(
            [
                total[p * each : (p + 1) * each],
                total[split + p * pool_dev : split + (p + 1) * pool_dev],
            ]
        )
        for p in STEPS
    ]
    own_sum = blocks[0].astype(F32)
    for p in STEPS[1:]:
        own_sum = own_sum + far_move(blocks[p], p).astype(F32)
    own_sum, back = lax.optimization_barrier((own_sum.astype(BF16), back))
    ent_grad = jnp.sum(back.astype(F32), axis=0).astype(BF16)

    sums = spread(own_sum, REP, REPS)
    rel_own = jnp.einsum(
        "gwab,akb->gwk",
        sums[:, :each].reshape(REPS, mine, rows_dev, feats),
        core,
        preferred_element_type=F32,
    ).astype(BF16)
    pool_own = jnp.sum(sums[:, each:].astype(F32), axis=0).astype(BF16)

    rel_rows = rels * feats_rel // feats
    small = spread(jnp.concatenate([rel_own.reshape(rel_rows, feats), pool_own]), LINE, Z)
    (core_grad,) = call(
        functools.partial(core_kernel, rows_dev),
        ((rows_dev, feats_rel, feats),),
        2 * rows_dev * feats_rel * rels * feats,
        [vmem] * 2,
        (pltpu.VMEM((feats // 128, rels * rows_dev, 128), F32),),
    )(ordered, sums)
    small, core_grad, ent_grad = lax.optimization_barrier((small, core_grad, ent_grad))
    rel_grad, pool_grad = call(
        last_kernel,
        ((rels, feats_rel), (pool_rows, feats)),
        1 << 20,
        [smem] + [vmem] * 3,
        dtypes=(F32, BF16),
    )(where, small, swap_core(small), order_sel)
    return (core_grad, rel_grad, ent_grad, pool_grad)


def solution(mesh):
    cut = Mesh(mesh.devices.reshape(ZH, ZL, CORES, 4, 4), REL + REP)
    whole = REL + REP
    return jax.shard_map(
        body,
        mesh=cut,
        in_specs=(
            P(REL, None, None),
            P(),
            P(whole, None),
            P(),
            P(),
            P(whole),
            P(whole),
            P(whole),
            P(whole, None),
        ),
        out_specs=(P(REL, None, None), P(), P(whole, None), P()),
        check_vma=False,
    )
```
